256 devices in a mesh: segment: 16 (over z_lo, y), expert: 16 (over x, z_hi, core).
Axes of the slice: x: 4, y: 4, z: 8 (z_hi: 2, z_lo: 4; z = z_hi * 4 + z_lo), core: 2. Of those that a mesh axis runs over, the one named last changes fastest.
Arguments:
- rising_acts: bfloat16 [16, 2048, 3584], P('segment', 'expert'), may hold values from -6 to 6
- falling_acts: bfloat16 [16, 2048, 3584], P('segment', 'expert'), may hold values from -6 to 6
- norm_gain: float32 [16, 3584], P('segment'), may hold values from 0.5 to 1.5
- router_weight: float32 [16, 3584, 4], P('segment'), may hold values from -0.1875 to 0.1875
- gate_weight: bfloat16 [16, 3584, 4096], P('segment', None, 'expert'), may hold values from -0.09375 to 0.09375
- up_weight: bfloat16 [16, 3584, 4096], P('segment', None, 'expert'), may hold values from -0.09375 to 0.09375
- down_weight: bfloat16 [16, 4096, 3584], P('segment', 'expert'), may hold values from -0.1875 to 0.1875
- rising_ids: int32 [16, 64, 2], P('segment', 'expert'), may hold values from 0 to 3, all different within a row; in each aligned block of 4 rows (0 to 3, 4 to 7, ..., all dimensions but the last counted through in order) at most 2 rows name the same one
- falling_ids: int32 [16, 64, 2], P('segment', 'expert'), may hold values from 0 to 3, all different within a row; in each aligned block of 4 rows (0 to 3, 4 to 7, ..., all dimensions but the last counted through in order) at most 2 rows name the same one
Outputs:
- rising_next: bfloat16 [16, 2048, 3584], P('segment', 'expert')
- falling_next: bfloat16 [16, 2048, 3584], P('segment', 'expert')
The draws below stay inside these ranges and needn't reach their ends.
Inputs may be any that keep to these rules, and one draw needn't show every extreme that they name: `rising_ids`: within the 4 blocks of one index of expert in one section, every expert is named by exactly 2 blocks. `falling_ids`: within the 4 blocks of one index of expert in one section, every expert is named by exactly 2 blocks.
All inputs are finite; a program needn't handle non-finite values.
Results may differ from the reference program's by a relative error of at most 0.009.
Values may be sent and summed in bfloat16 or wider, within the bound.
A program may use at most 128 MiB of HBM per device.

```python
import math
import jax
import jax.numpy as jnp
import numpy as np
from jax import lax

D = 3584
FF = 1024
E = 4
TOP = 2
BLOCK = 32
CAP = 2
BLK_DEV = 4
SEGMENTS = 16
BLOCKS = 64
TOKENS = 2048
GROUP = 4
FF_DEV = 256
N_EXPERT = 16


def level_of(stream_key, shape, split, low, top_value):
    def one(axis_at, shards_of):
        heights = jax.random.uniform(jax.random.fold_in(jax.random.fold_in(stream_key, 6), axis_at), (shards_of,), jnp.float32, low / len(split), top_value / len(split))
        return jnp.repeat(jnp.exp(heights), shape[axis_at] // shards_of).reshape((-1,) + (1,) * (len(shape) - axis_at - 1))

    gain = one(*split[0])
    for cut in split[1:]:
        gain = gain * one(*cut)
    return gain


def shared_out(rng, own, number, rows, number_of, top, reach, lean):
    order = jax.random.permutation(rng, number_of)
    heavy_load, common = load_shares(number_of, rows * top, reach, lean, True), load_shares(number_of, rows * top, reach, lean, False)
    places = jnp.arange(number_of)

    def named(lengths, offset_by):
        used = int((lengths > 0).sum())
        fixed = max(1, used // 4)
        passed = fixed + (places - fixed + offset_by * (used - fixed)) % max(1, number_of - fixed)
        return jnp.zeros((number_of,), jnp.int32).at[order[jnp.where(places < fixed, places, passed)]].set(jnp.asarray(lengths, jnp.int32))

    lengths = jnp.where(number % 4 == 0, named(heavy_load, number // 4), named(common, number - number // 4 - 1))
    mixed = jax.random.permutation(jax.random.fold_in(own, 3), number_of)
    donor, taker = mixed[0:number_of // 2 * 2:2], mixed[1:number_of // 2 * 2:2]
    margin = jnp.minimum(lengths[donor] - 1, reach - lengths[taker]) // 2
    margin = jnp.where((donor == order[0]) | (taker == order[0]) | (lengths[taker] == 0), 0, jnp.maximum(margin, 0))
    passed = jax.random.randint(jax.random.fold_in(own, 4), (number_of // 2,), 0, 1 << 20) % (margin + 1)
    lengths = lengths.at[donor].add(-passed).at[taker].add(passed)
    items = jnp.searchsorted(jnp.cumsum(lengths), jnp.arange(rows * top), side="right").astype(jnp.int32)
    grid = items.reshape(top, rows).T
    grid = grid[jax.random.permutation(jax.random.fold_in(own, 1), rows)]
    offset_by = jax.random.randint(jax.random.fold_in(own, 2), (rows, 1), 0, top)
    return jnp.take_along_axis(grid, (jnp.arange(top)[None, :] + offset_by) % top, axis=1)


def load_shares(number_of, total, most, slope, full):
    weights = [(1 << 20) // math.isqrt(standing ** slope) + 1 for standing in range(1, number_of + 1)]
    largest = most if full else min(most, max(-(-total // number_of), total * weights[0] // sum(weights)))
    least = 1 if total - largest >= number_of - 1 else 0
    counts, spare = [largest] + [least] * (number_of - 1), total - largest - least * (number_of - 1)
    while spare > 0:
        free = [i for i in range(1, number_of) if counts[i] < largest] or [i for i in range(1, number_of) if counts[i] < most]
        pool, left = sum([weights[i] for i in free]), spare
        for i in free:
            more = min(most - counts[i], max(1, left * weights[i] // pool), spare)
            counts[i] = counts[i] + more
            spare = spare - more
    return np.array(counts)


def normal_values(own_key, dims, width, limit, cuts=(), held_as=jnp.bfloat16):
    drawn = width * jax.random.normal(own_key, dims, jnp.float32)
    if cuts:
        drawn = drawn * level_of(own_key, dims, cuts, -0.22, 0.18)
    return jnp.clip(drawn, -limit, limit).astype(held_as)


def setup_inputs(seed: int = 0) -> dict:
    keys = jax.random.split(jax.random.key(seed), 10)
    rising_acts = normal_values(keys[0], (SEGMENTS, TOKENS, D), 1.0, 6.0, ((0, 16), (1, 16)))
    falling_acts = normal_values(keys[1], (SEGMENTS, TOKENS, D), 1.0, 6.0, ((0, 16), (1, 16)))
    norm_gain = jnp.clip(1.0 + 0.1 * jax.random.normal(keys[2], (SEGMENTS, D), jnp.float32), 0.5, 1.5)
    router_weight = normal_values(keys[3], (SEGMENTS, D, E), (D // 4) ** -0.5, 0.1875, ((0, 16),), jnp.float32)
    gate_weight = normal_values(keys[4], (SEGMENTS, D, E * FF), D ** -0.5, 0.09375, ((0, 16), (2, 16)))
    up_weight = normal_values(keys[5], (SEGMENTS, D, E * FF), D ** -0.5, 0.09375, ((0, 16), (2, 16)))
    down_weight = normal_values(keys[6], (SEGMENTS, E * FF, D), FF ** -0.5, 0.1875, ((0, 16), (1, 16)))
    rising_ids_keys = jax.random.split(jax.random.fold_in(keys[7], 1), SEGMENTS * BLOCKS // BLK_DEV)
    rising_ids_turns = jax.random.permutation(jax.random.fold_in(keys[7], 3), SEGMENTS * BLOCKS // BLK_DEV)
    rising_ids = jax.vmap(lambda own, number: shared_out(jax.random.fold_in(keys[7], 2), own, number, BLK_DEV, E, TOP, CAP, 0))(rising_ids_keys, rising_ids_turns).reshape((SEGMENTS, BLOCKS, TOP))
    falling_ids_keys = jax.random.split(jax.random.fold_in(keys[8], 1), SEGMENTS * BLOCKS // BLK_DEV)
    falling_ids_turns = jax.random.permutation(jax.random.fold_in(keys[8], 3), SEGMENTS * BLOCKS // BLK_DEV)
    falling_ids = jax.vmap(lambda own, number: shared_out(jax.random.fold_in(keys[8], 2), own, number, BLK_DEV, E, TOP, CAP, 0))(falling_ids_keys, falling_ids_turns).reshape((SEGMENTS, BLOCKS, TOP))
    return dict(rising_acts=rising_acts, falling_acts=falling_acts, norm_gain=norm_gain, router_weight=router_weight, gate_weight=gate_weight, up_weight=up_weight, down_weight=down_weight, rising_ids=rising_ids, falling_ids=falling_ids)


eps = 1e-06
route_scale = 2.5

def normalize(acts, gain_row):
    widened = acts.astype(jnp.float32)
    square_mean = lax.optimization_barrier(jnp.mean(widened * widened, axis=-1, keepdims=True))
    return (widened * lax.rsqrt(square_mean + eps) * gain_row).astype(jnp.bfloat16)

def combine_parts(parts):
    if len(parts) == 1:
        return parts[0].astype(jnp.float32)
    level = list(parts)
    for level_index in range(max(len(parts).bit_length() - 2, 0)):
        level = [lax.optimization_barrier((level[2 * k].astype(jnp.float32) + level[2 * k + 1].astype(jnp.float32)).astype(jnp.bfloat16)) for k in range(len(level) // 2)]
    return level[0].astype(jnp.float32) + level[1].astype(jnp.float32)

def section(acts, gain_row, router, gate_slab, up_slab, down_slab, route_ids):
    normed = normalize(acts, gain_row)
    scores = jax.nn.sigmoid(jnp.dot(normed.astype(jnp.float32), router, precision=lax.Precision.HIGHEST))
    chosen_int = jnp.any(route_ids[:, :, None] == jnp.arange(E, dtype=jnp.int32)[None, None, :], axis=1).astype(jnp.int32)
    chosen = chosen_int.astype(jnp.float32)
    weighted = scores.reshape(BLOCKS, BLOCK, E) * chosen[:, None, :]
    gate_share = weighted / lax.optimization_barrier(jnp.sum(weighted, axis=-1, keepdims=True))
    normed_blocks = normed.reshape(N_EXPERT, BLK_DEV, BLOCK, D).astype(jnp.float32)
    chosen_dev = chosen_int.reshape(N_EXPERT, BLK_DEV, E)
    slot_rank = jnp.cumsum(chosen_dev, axis=1).astype(jnp.int32) - chosen_dev
    slot_ids = jnp.arange(CAP, dtype=jnp.int32)
    selector = (chosen_dev[..., None] * (slot_rank[..., None] == slot_ids).astype(jnp.int32)).astype(jnp.float32)
    mixing = gate_share.reshape(N_EXPERT, BLK_DEV, BLOCK, E)
    contribution = jnp.zeros((N_EXPERT, BLK_DEV, BLOCK, D), jnp.float32)
    for expert in range(E):
        select_e = selector[:, :, expert, :]
        picked = jnp.einsum('sbc,sbrd->scrd', select_e, normed_blocks).astype(jnp.bfloat16).reshape(N_EXPERT * CAP * BLOCK, D)
        first = expert * FF
        gate_pre = jnp.dot(picked, gate_slab[:, first:first + FF], preferred_element_type=jnp.float32)
        up_pre = jnp.dot(picked, up_slab[:, first:first + FF], preferred_element_type=jnp.float32)
        hidden = (jax.nn.silu(gate_pre) * up_pre).astype(jnp.bfloat16)
        parts = []
        for member in range(GROUP):
            start = first + member * FF_DEV
            partial_value = jnp.dot(hidden[:, member * FF_DEV:(member + 1) * FF_DEV], down_slab[start:start + FF_DEV], preferred_element_type=jnp.float32).astype(jnp.bfloat16)
            parts.append(lax.optimization_barrier(partial_value))
        total = combine_parts(parts)
        returned = jnp.einsum('sbc,scrd->sbrd', select_e, total.reshape(N_EXPERT, CAP, BLOCK, D))
        contribution = contribution + mixing[..., expert][..., None] * returned
    widened = acts.astype(jnp.float32).reshape(N_EXPERT, BLK_DEV, BLOCK, D)
    return (widened + route_scale * contribution).reshape(TOKENS, D).astype(jnp.bfloat16)

def reference(rising_acts, falling_acts, norm_gain, router_weight, gate_weight, up_weight, down_weight, rising_ids, falling_ids):

    def one_segment(inputs):
        rising, falling, gain_row, router, gate_slab, up_slab, down_slab, rising_route, falling_route = inputs
        rising_out = section(rising, gain_row, router, gate_slab, up_slab, down_slab, rising_route)
        falling_out = section(falling, gain_row, router, gate_slab, up_slab, down_slab, falling_route)
        return (rising_out, falling_out)
    rising_all, falling_all = lax.map(one_segment, (rising_acts, falling_acts, norm_gain, router_weight, gate_weight, up_weight, down_weight, rising_ids, falling_ids))
    return (jnp.roll(rising_all, 1, axis=0), jnp.roll(falling_all, -1, axis=0))
```

```python
import functools

import jax
import jax.numpy as jnp
from jax import lax
from jax.experimental import pallas as pl
from jax.experimental.pallas import tpu as pltpu
from jax.sharding import PartitionSpec as P

MESH = pl.DeviceIdType.MESH
EPS = 1e-06
ROUTE_SCALE = 2.5
EXPERTS = 4
XN = 4
CHUNKS = 4
BR = 32
LANES = 128
F32 = jnp.float32
BF16 = jnp.bfloat16


def relay_kernel(
    rows,
    features,
    units,
    segments,
    rise_hbm,
    fall_hbm,
    gain_ref,
    router_ref,
    gate_hbm,
    up_hbm,
    down_hbm,
    ids_hbm,
    rise_out,
    fall_out,
    acts,
    gate_w,
    up_w,
    down_w,
    ids_own,
    ids_land,
    ids_far,
    picker,
    mixer,
    mixer_rest,
    normed,
    far_normed,
    sending,
    arrived,
    hidden,
    core_sum,
    returned,
    z_out,
    z_in,
    finished,
    scores,
    act_sem,
    w_sem,
    dw_sem,
    ids_sem,
    ids_ss,
    ids_rs,
    zf_ss,
    zf_rs,
    xf_ss,
    xf_rs,
    df_ss,
    df_rs,
    dp_ss,
    dp_rs,
    xr_ss,
    xr_rs,
    zr_ss,
    zr_rs,
    y_ss,
    y_rs,
):
    width = features // CHUNKS
    pick_rows = 2 * BR
    half = XN * pick_rows
    blocks = rows // BR
    tiles = width // LANES

    seg = lax.axis_index("segment")
    me = lax.axis_index("expert")
    x = me // 4
    core = lax.rem(me, 2)
    z_hi = lax.rem(me // 2, 2)
    z_mate = me + 2 - 4 * z_hi
    core_mate = me + 1 - 2 * core
    seg_up = lax.rem(seg + 1, segments)
    seg_down = lax.rem(seg + segments - 1, segments)
    own_half = pl.multiple_of(core * half, half)
    mate_half = pl.multiple_of((1 - core) * half, half)

    def x_at(i):
        return lax.rem(x + i, XN)

    def x_device(i):
        return me + 4 * (x_at(i) - x)

    def z_forward(mb, k):
        return pltpu.make_async_remote_copy(
            src_ref=normed.at[mb, k],
            dst_ref=far_normed.at[mb, k],
            send_sem=zf_ss.at[mb, k],
            recv_sem=zf_rs.at[mb, k],
            device_id=(seg, z_mate),
            device_id_type=MESH,
        )

    def x_forward(s, k, i):
        return pltpu.make_async_remote_copy(
            src_ref=sending.at[s, k, pl.ds(pl.multiple_of(x_at(i) * pick_rows, pick_rows), pick_rows)],
            dst_ref=arrived.at[s, k, pl.ds(pl.multiple_of(own_half + x * pick_rows, pick_rows), pick_rows)],
            send_sem=xf_ss.at[s, k, i - 1],
            recv_sem=xf_rs.at[s, k, i - 1],
            device_id=(seg, x_device(i)),
            device_id_type=MESH,
        )

    def core_forward(s, k):
        return pltpu.make_async_remote_copy(
            src_ref=arrived.at[s, k, pl.ds(own_half, half)],
            dst_ref=arrived.at[s, k, pl.ds(own_half, half)],
            send_sem=df_ss.at[s, k],
            recv_sem=df_rs.at[s, k],
            device_id=(seg, core_mate),
            device_id_type=MESH,
        )

    def core_part(s, k):
        return pltpu.make_async_remote_copy(
            src_ref=arrived.at[s, k, pl.ds(mate_half, half)],
            dst_ref=core_sum.at[s, k],
            send_sem=dp_ss.at[s, k],
            recv_sem=dp_rs.at[s, k],
            device_id=(seg, core_mate),
            device_id_type=MESH,
        )

    def x_return(s, k, i):
        return pltpu.make_async_remote_copy(
            src_ref=arrived.at[s, k, pl.ds(pl.multiple_of(own_half + x_at(i) * pick_rows, pick_rows), pick_rows)],
            dst_ref=returned.at[s, k, pl.ds(pl.multiple_of(x * pick_rows, pick_rows), pick_rows)],
            send_sem=xr_ss.at[s, k, i - 1],
            recv_sem=xr_rs.at[s, k, i - 1],
            device_id=(seg, x_device(i)),
            device_id_type=MESH,
        )

    def z_return(mb, k):
        return pltpu.make_async_remote_copy(
            src_ref=z_out.at[mb, k],
            dst_ref=z_in.at[mb, k],
            send_sem=zr_ss.at[mb, k],
            recv_sem=zr_rs.at[mb, k],
            device_id=(seg, z_mate),
            device_id_type=MESH,
        )

    def shift(mb, k):
        out = rise_out if mb == 0 else fall_out
        return pltpu.make_async_remote_copy(
            src_ref=finished.at[mb, k],
            dst_ref=out.at[0, :, pl.ds(k * width, width)],
            send_sem=y_ss.at[mb, k],
            recv_sem=y_rs.at[mb, k],
            device_id=(seg_up if mb == 0 else seg_down, me),
            device_id_type=MESH,
        )

    ids_exchange = pltpu.make_async_remote_copy(
        src_ref=ids_hbm,
        dst_ref=ids_land,
        send_sem=ids_ss,
        recv_sem=ids_rs,
        device_id=(seg, z_mate),
        device_id_type=MESH,
    )

    def normalize(mb):
        @pl.loop(0, blocks)
        def _(b):
            at = pl.ds(pl.multiple_of(b * BR, BR), BR)
            value = acts[mb, at, :].astype(F32)
            scale = lax.rsqrt(jnp.mean(value * value, axis=-1, keepdims=True) + EPS)
            for k in range(CHUNKS):
                cut = slice(k * width, (k + 1) * width)
                normed[mb, k, at, :] = (value[:, cut] * scale * gain_ref[:, cut]).astype(BF16)

    def codes(s, ids):
        mb = s % 2
        named = [[ids[2 * mb + j, b] for j in range(2)] for b in range(blocks)]
        code = []
        for b in range(blocks):
            code.append([])
            for j in range(2):
                slot = jnp.int32(0)
                for earlier in range(b):
                    for other in range(2):
                        slot = slot + (named[earlier][other] == named[b][j]).astype(jnp.int32)
                code[b].append(2 * named[b][j] + slot)
        return named, code

    def set_picker(s, ids):
        _, code = codes(s, ids)
        row = lax.broadcasted_iota(jnp.int32, (half, rows), 0)
        column = lax.broadcasted_iota(jnp.int32, (half, rows), 1)
        same = (row % BR == column % BR).astype(F32)
        total = jnp.zeros((half, rows), F32)
        for j in range(2):
            wanted = jnp.zeros((half, rows), jnp.int32)
            for b in range(blocks):
                wanted = wanted + (column // BR == b).astype(jnp.int32) * code[b][j]
            total = total + (row // BR == wanted).astype(F32)
        picker[s] = (total * same).astype(BF16)

    def pick(s, k):
        source = normed if s < 2 else far_normed
        chosen = jnp.dot(picker[s], source[s % 2, k], preferred_element_type=F32)
        sending[s, k] = chosen.astype(BF16)
        own = pl.ds(pl.multiple_of(x * pick_rows, pick_rows), pick_rows)
        mine = pl.ds(pl.multiple_of(own_half + x * pick_rows, pick_rows), pick_rows)
        arrived[s, k, mine, :] = sending[s, k, own, :]
        for i in range(1, XN):
            x_forward(s, k, i).start()

    def relay(s, k):
        z_forward(s % 2, k).wait_recv()
        pick(s, k)

    def gates(s, ids):
        source = normed if s < 2 else far_normed
        mb = s % 2

        @pl.loop(0, blocks)
        def _(b):
            at = pl.ds(pl.multiple_of(b * BR, BR), BR)
            sums = [jnp.zeros((BR, LANES), F32) for _ in range(EXPERTS)]
            for k in range(CHUNKS):
                for t in range(tiles):
                    value = source[mb, k, at, t * LANES : (t + 1) * LANES].astype(F32)
                    first = k * width + t * LANES
                    for e in range(EXPERTS):
                        sums[e] = sums[e] + value * router_ref[e : e + 1, first : first + LANES]
            for e in range(EXPERTS):
                total = jnp.sum(sums[e], axis=-1, keepdims=True)
                scores[e, at, :] = jnp.broadcast_to(jax.nn.sigmoid(total), (BR, LANES))

        named, code = codes(s, ids)
        column = lax.broadcasted_iota(jnp.int32, (BR, LANES), 1)
        row = lax.broadcasted_iota(jnp.int32, (BR, LANES), 0)
        same = (column % BR == row).astype(F32)
        for b in range(blocks):
            at = slice(b * BR, (b + 1) * BR)
            score = []
            for j in range(2):
                value = jnp.zeros((BR, LANES), F32)
                for e in range(EXPERTS):
                    value = value + scores[e, at, :] * (named[b][j] == e).astype(F32)
                score.append(value)
            total = score[0] + score[1]
            for first in range(0, half, LANES):
                place = (column + first) // BR
                value = jnp.zeros((BR, LANES), F32)
                for j in range(2):
                    value = value + (place == code[b][j]).astype(F32) * same * (score[j] / total)
                main = value.astype(BF16)
                mixer[s, at, first : first + LANES] = main
                mixer_rest[s, at, first : first + LANES] = (value - main.astype(F32)).astype(BF16)

    def to_core(s, k):
        for i in range(1, XN):
            x_forward(s, k, i).wait_recv()
        core_forward(s, k).start()

    def experts(s):
        for k in range(CHUNKS):
            core_forward(s, k).wait_recv()
            core_forward(s, k).wait_send()

        @pl.loop(0, 2)
        def _(t):
            at = pl.ds(pl.multiple_of(t * half, half), half)
            gate_pre = jnp.zeros((half, units), F32)
            up_pre = jnp.zeros((half, units), F32)
            for k in range(CHUNKS):
                value = arrived[s, k, at, :]
                cut = slice(k * width, (k + 1) * width)
                gate_pre = gate_pre + jnp.dot(value, gate_w[cut, :], preferred_element_type=F32)
                up_pre = up_pre + jnp.dot(value, up_w[cut, :], preferred_element_type=F32)
            hidden[at, :] = (jax.nn.silu(gate_pre) * up_pre).astype(BF16)

        @pl.loop(0, CHUNKS)
        def _(k):
            for first in (mate_half, own_half):
                at = pl.ds(first, half)
                part = jnp.dot(hidden[at, :], down_w[k], preferred_element_type=F32)
                arrived[s, k, at, :] = part.astype(BF16)
                if first is mate_half:
                    core_part(s, k).start()

    def pair_sum(s, k):
        core_part(s, k).wait_recv()

        @pl.loop(0, XN)
        def _(i):
            at = pl.ds(pl.multiple_of(i * pick_rows, pick_rows), pick_rows)
            mine = pl.ds(pl.multiple_of(own_half + i * pick_rows, pick_rows), pick_rows)
            total = arrived[s, k, mine, :].astype(F32) + core_sum[s, k, at, :].astype(F32)
            arrived[s, k, mine, :] = total.astype(BF16)

        here = pl.ds(pl.multiple_of(x * pick_rows, pick_rows), pick_rows)
        mine = pl.ds(pl.multiple_of(own_half + x * pick_rows, pick_rows), pick_rows)
        returned[s, k, here, :] = arrived[s, k, mine, :]

    def send_back(s, k):
        for i in range(1, XN):
            x_return(s, k, i).start()

    def weighted(s, k):
        value = returned[s, k]
        return jnp.dot(mixer[s], value, preferred_element_type=F32) + jnp.dot(
            mixer_rest[s], value, preferred_element_type=F32
        )

    def combine(s, k):
        mb = s % 2
        for i in range(1, XN):
            x_return(s, k, i).wait_recv()
        z_out[mb, k] = weighted(s, k).astype(BF16)
        z_return(mb, k).start()

    def finish(mb, k):
        for i in range(1, XN):
            x_return(mb, k, i).wait_recv()
        z_return(mb, k).wait_recv()
        total = weighted(mb, k) + z_in[mb, k].astype(F32)
        mixed = acts[mb, :, k * width : (k + 1) * width].astype(F32) + ROUTE_SCALE * total
        finished[mb, k] = mixed.astype(BF16)
        shift(mb, k).start()

    act_copies = [
        pltpu.make_async_copy(source.at[0], acts.at[mb], act_sem.at[mb])
        for mb, source in enumerate((rise_hbm, fall_hbm))
    ]
    weight_copies = [
        pltpu.make_async_copy(gate_hbm.at[0], gate_w, w_sem.at[0]),
        pltpu.make_async_copy(up_hbm.at[0], up_w, w_sem.at[1]),
    ] + [
        pltpu.make_async_copy(down_hbm.at[0, :, pl.ds(k * width, width)], down_w.at[k], dw_sem.at[k])
        for k in range(CHUNKS)
    ]
    ids_copy = pltpu.make_async_copy(ids_hbm, ids_own, ids_sem.at[0])
    act_copies[0].start()
    ids_copy.start()
    act_copies[1].start()
    for copy in weight_copies:
        copy.start()

    barrier = pltpu.get_barrier_semaphore()
    partners = [(seg, x_device(i)) for i in range(1, XN)]
    partners += [(seg, z_mate), (seg, core_mate), (seg_up, me), (seg_down, me)]
    for partner in partners:
        pl.semaphore_signal(barrier, inc=1, device_id=partner, device_id_type=MESH)

    act_copies[0].wait()
    normalize(0)
    ids_copy.wait()
    set_picker(0, ids_own)
    pl.semaphore_wait(barrier, len(partners))

    every = range(CHUNKS)
    rise, fall, far_rise, far_fall = range(4)
    for k in every:
        z_forward(0, k).start()
    ids_exchange.start()
    for k in every:
        pick(rise, k)
    set_picker(fall, ids_own)
    act_copies[1].wait()
    normalize(1)
    for k in every:
        z_forward(1, k).start()
    gates(rise, ids_own)
    ids_exchange.wait()
    ids_far_copy = pltpu.make_async_copy(ids_land, ids_far, ids_sem.at[1])
    ids_far_copy.start()
    ids_far_copy.wait()
    set_picker(far_rise, ids_far)
    set_picker(far_fall, ids_far)
    to_core(rise, 0)
    relay(far_rise, 0)
    pick(fall, 0)
    for k in every[1:]:
        to_core(rise, k)
    for copy in weight_copies:
        copy.wait()
    experts(rise)
    for k in every[1:]:
        relay(far_rise, k)
        pick(fall, k)
    for k in every:
        pair_sum(rise, k)
    gates(fall, ids_own)
    for k in every:
        to_core(far_rise, k)
        to_core(fall, k)
    experts(far_rise)
    for k in every:
        pair_sum(far_rise, k)
        send_back(far_rise, k)
    gates(far_rise, ids_far)
    for k in every[: CHUNKS // 2]:
        relay(far_fall, k)
    experts(fall)
    for k in every:
        pair_sum(fall, k)
    for k in every[: CHUNKS // 2]:
        combine(far_rise, k)
    for k in every[CHUNKS // 2 :]:
        relay(far_fall, k)
        combine(far_rise, k)
    gates(far_fall, ids_far)
    for k in every[: CHUNKS // 2]:
        send_back(rise, k)
    for k in every:
        to_core(far_fall, k)
    experts(far_fall)
    for k in every:
        pair_sum(far_fall, k)
        send_back(far_fall, k)
    for k in every[CHUNKS // 2 :]:
        send_back(rise, k)
    for k in every:
        send_back(fall, k)
    for k in every[: CHUNKS // 2]:
        finish(0, k)
    for k in every:
        combine(far_fall, k)
    for k in every[CHUNKS // 2 :]:
        finish(0, k)
    for k in every:
        finish(1, k)

    for k in every:
        for mb in range(2):
            z_forward(mb, k).wait_send()
            z_return(mb, k).wait_send()
            shift(mb, k).wait_send()
        for s in range(4):
            core_part(s, k).wait_send()
            for i in range(1, XN):
                x_forward(s, k, i).wait_send()
                x_return(s, k, i).wait_send()
    for k in every:
        for mb in range(2):
            shift(mb, k).wait_recv()


def on_device(
    rising_acts,
    falling_acts,
    norm_gain,
    router_weight,
    gate_weight,
    up_weight,
    down_weight,
    rising_ids,
    falling_ids,
):
    rows, features = rising_acts.shape[1:]
    units = gate_weight.shape[2]
    width = features // CHUNKS
    half = XN * 2 * BR
    segments = lax.axis_size("segment")
    named = jnp.concatenate([rising_ids[0].T, falling_ids[0].T], axis=0)
    ids = jnp.pad(named, ((0, 8 - named.shape[0]), (0, LANES - named.shape[1])))
    dma = pltpu.SemaphoreType.DMA
    hbm = pl.BlockSpec(memory_space=pl.ANY)
    vmem = pl.BlockSpec(memory_space=pltpu.VMEM)
    result = jax.ShapeDtypeStruct(rising_acts.shape, BF16)
    return pl.pallas_call(
        functools.partial(relay_kernel, rows, features, units, segments),
        out_shape=(result, result),
        in_specs=[hbm, hbm, vmem, vmem, hbm, hbm, hbm, hbm],
        out_specs=(hbm, hbm),
        scratch_shapes=[
            pltpu.VMEM((2, rows, features), BF16),
            pltpu.VMEM((features, units), BF16),
            pltpu.VMEM((features, units), BF16),
            pltpu.VMEM((CHUNKS, units, width), BF16),
            pltpu.SMEM((8, LANES), jnp.int32),
            pltpu.VMEM((8, LANES), jnp.int32),
            pltpu.SMEM((8, LANES), jnp.int32),
            pltpu.VMEM((4, half, rows), BF16),
            pltpu.VMEM((4, rows, half), BF16),
            pltpu.VMEM((4, rows, half), BF16),
            pltpu.VMEM((2, CHUNKS, rows, width), BF16),
            pltpu.VMEM((2, CHUNKS, rows, width), BF16),
            pltpu.VMEM((4, CHUNKS, half, width), BF16),
            pltpu.VMEM((4, CHUNKS, 2 * half, width), BF16),
            pltpu.VMEM((2 * half, units), BF16),
            pltpu.VMEM((4, CHUNKS, half, width), BF16),
            pltpu.VMEM((4, CHUNKS, half, width), BF16),
            pltpu.VMEM((2, CHUNKS, rows, width), BF16),
            pltpu.VMEM((2, CHUNKS, rows, width), BF16),
            pltpu.VMEM((2, CHUNKS, rows, width), BF16),
            pltpu.VMEM((EXPERTS, rows, LANES), F32),
            dma((2,)),
            dma((2,)),
            dma((CHUNKS,)),
            dma((2,)),
            dma,
            dma,
            dma((2, CHUNKS)),
            dma((2, CHUNKS)),
            dma((4, CHUNKS, XN - 1)),
            dma((4, CHUNKS, XN - 1)),
            dma((4, CHUNKS)),
            dma((4, CHUNKS)),
            dma((4, CHUNKS)),
            dma((4, CHUNKS)),
            dma((4, CHUNKS, XN - 1)),
            dma((4, CHUNKS, XN - 1)),
            dma((2, CHUNKS)),
            dma((2, CHUNKS)),
            dma((2, CHUNKS)),
            dma((2, CHUNKS)),
        ],
        compiler_params=pltpu.CompilerParams(
            collective_id=0, has_side_effects=True, vmem_limit_bytes=60 << 20
        ),
        name="relay",
    )(
        rising_acts,
        falling_acts,
        norm_gain,
        router_weight[0].T,
        gate_weight,
        up_weight,
        down_weight,
        ids,
    )


def solution(mesh):
    return jax.shard_map(
        on_device,
        mesh=mesh,
        in_specs=(
            P("segment", "expert", None),
            P("segment", "expert", None),
            P("segment", None),
            P("segment", None, None),
            P("segment", None, "expert"),
            P("segment", None, "expert"),
            P("segment", "expert", None),
            P("segment", "expert", None),
            P("segment", "expert", None),
        ),
        out_specs=(P("segment", "expert", None), P("segment", "expert", None)),
        check_vma=False,
    )
```

```python
import functools

import jax
import jax.numpy as jnp
from jax import lax
from jax.experimental import pallas as pl
from jax.experimental.pallas import tpu as pltpu
from jax.sharding import PartitionSpec as P

MESH = pl.DeviceIdType.MESH
EPS = 1e-06
ROUTE_SCALE = 2.5
EXPERTS = 4
XN = 4
CHUNKS = 7
FILL = (2, 5)
YN = 4
DETOURS = ((1, 2, 0, 1, 2), (2, 1, 3, 2, 1))
BR = 32
LANES = 128
F32 = jnp.float32
BF16 = jnp.bfloat16


def relay_kernel(
    rows,
    features,
    units,
    segments,
    rise_hbm,
    fall_hbm,
    gain_ref,
    router_ref,
    gate_hbm,
    up_hbm,
    down_hbm,
    ids_hbm,
    rise_out,
    fall_out,
    acts,
    gate_w,
    up_w,
    down_w,
    ids_own,
    ids_land,
    ids_far,
    picker,
    mixer,
    mixer_rest,
    normed,
    far_normed,
    sending,
    arrived,
    hidden,
    core_sum,
    returned,
    z_out,
    z_in,
    finished,
    scores,
    act_sem,
    w_sem,
    dw_sem,
    ids_sem,
    ids_ss,
    ids_rs,
    zf_ss,
    zf_rs,
    xf_ss,
    xf_rs,
    df_ss,
    df_rs,
    dp_ss,
    dp_rs,
    xr_ss,
    xr_rs,
    zr_ss,
    zr_rs,
    y_ss,
    y_rs,
    passing,
    pass_ss,
    pass_rs,
):
    width = features // CHUNKS
    pick_rows = 2 * BR
    half = XN * pick_rows
    blocks = rows // BR
    tiles = width // LANES

    seg = lax.axis_index("segment")
    me = lax.axis_index("expert")
    x = me // 4
    core = lax.rem(me, 2)
    z_hi = lax.rem(me // 2, 2)
    z_mate = me + 2 - 4 * z_hi
    core_mate = me + 1 - 2 * core
    seg_up = lax.rem(seg + 1, segments)
    seg_down = lax.rem(seg + segments - 1, segments)
    y = lax.rem(seg, YN)
    z_lo = seg // YN
    z_count = segments // YN
    seg_base = seg - y
    base_up = lax.rem(z_lo + 1, z_count) * YN
    base_down = lax.rem(z_lo + z_count - 1, z_count) * YN
    at_edge = (y == YN - 1, y == 0)
    past_edge = (base_up, base_down + YN - 1)
    own_half = pl.multiple_of(core * half, half)
    mate_half = pl.multiple_of((1 - core) * half, half)

    def x_at(i):
        return lax.rem(x + i, XN)

    def x_device(i):
        return me + 4 * (x_at(i) - x)

    def z_forward(mb, k):
        return pltpu.make_async_remote_copy(
            src_ref=normed.at[mb, k],
            dst_ref=far_normed.at[mb, k],
            send_sem=zf_ss.at[mb, k],
            recv_sem=zf_rs.at[mb, k],
            device_id=(seg, z_mate),
            device_id_type=MESH,
        )

    def x_forward(s, k, i):
        return pltpu.make_async_remote_copy(
            src_ref=sending.at[s, k, pl.ds(pl.multiple_of(x_at(i) * pick_rows, pick_rows), pick_rows)],
            dst_ref=arrived.at[s, k, pl.ds(pl.multiple_of(own_half + x * pick_rows, pick_rows), pick_rows)],
            send_sem=xf_ss.at[s, k, i - 1],
            recv_sem=xf_rs.at[s, k, i - 1],
            device_id=(seg, x_device(i)),
            device_id_type=MESH,
        )

    def core_forward(s, k):
        return pltpu.make_async_remote_copy(
            src_ref=arrived.at[s, k, pl.ds(own_half, half)],
            dst_ref=arrived.at[s, k, pl.ds(own_half, half)],
            send_sem=df_ss.at[s, k],
            recv_sem=df_rs.at[s, k],
            device_id=(seg, core_mate),
            device_id_type=MESH,
        )

    def core_part(s, k):
        return pltpu.make_async_remote_copy(
            src_ref=arrived.at[s, k, pl.ds(mate_half, half)],
            dst_ref=core_sum.at[s, k],
            send_sem=dp_ss.at[s, k],
            recv_sem=dp_rs.at[s, k],
            device_id=(seg, core_mate),
            device_id_type=MESH,
        )

    def x_return(s, k, i):
        return pltpu.make_async_remote_copy(
            src_ref=arrived.at[s, k, pl.ds(pl.multiple_of(own_half + x_at(i) * pick_rows, pick_rows), pick_rows)],
            dst_ref=returned.at[s, k, pl.ds(pl.multiple_of(x * pick_rows, pick_rows), pick_rows)],
            send_sem=xr_ss.at[s, k, i - 1],
            recv_sem=xr_rs.at[s, k, i - 1],
            device_id=(seg, x_device(i)),
            device_id_type=MESH,
        )

    def z_return(mb, k):
        return pltpu.make_async_remote_copy(
            src_ref=z_out.at[mb, k],
            dst_ref=z_in.at[mb, k],
            send_sem=zr_ss.at[mb, k],
            recv_sem=zr_rs.at[mb, k],
            device_id=(seg, z_mate),
            device_id_type=MESH,
        )

    def shift(mb, k):
        out = rise_out if mb == 0 else fall_out
        return pltpu.make_async_remote_copy(
            src_ref=finished.at[mb, k],
            dst_ref=out.at[0, :, pl.ds(k * width, width)],
            send_sem=y_ss.at[mb, k],
            recv_sem=y_rs.at[mb, k],
            device_id=(seg_up if mb == 0 else seg_down, me),
            device_id_type=MESH,
        )

    def detour(mb, k):
        return pltpu.make_async_remote_copy(
            src_ref=finished.at[mb, k],
            dst_ref=passing.at[mb, k],
            send_sem=y_ss.at[mb, k],
            recv_sem=pass_rs.at[mb, k],
            device_id=(seg_base + DETOURS[mb][k], me),
            device_id_type=MESH,
        )

    def onward(mb, k):
        out = rise_out if mb == 0 else fall_out
        return pltpu.make_async_remote_copy(
            src_ref=passing.at[mb, k],
            dst_ref=out.at[0, :, pl.ds(k * width, width)],
            send_sem=pass_ss.at[mb, k],
            recv_sem=y_rs.at[mb, k],
            device_id=(past_edge[mb], me),
            device_id_type=MESH,
        )

    ids_exchange = pltpu.make_async_remote_copy(
        src_ref=ids_hbm,
        dst_ref=ids_land,
        send_sem=ids_ss,
        recv_sem=ids_rs,
        device_id=(seg, z_mate),
        device_id_type=MESH,
    )

    def normalize(mb):
        @pl.loop(0, blocks)
        def _(b):
            at = pl.ds(pl.multiple_of(b * BR, BR), BR)
            value = acts[mb, at, :].astype(F32)
            scale = lax.rsqrt(jnp.mean(value * value, axis=-1, keepdims=True) + EPS)
            for k in range(CHUNKS):
                cut = slice(k * width, (k + 1) * width)
                normed[mb, k, at, :] = (value[:, cut] * scale * gain_ref[:, cut]).astype(BF16)

    def codes(s, ids):
        mb = s % 2
        named = [[ids[2 * mb + j, b] for j in range(2)] for b in range(blocks)]
        code = []
        for b in range(blocks):
            code.append([])
            for j in range(2):
                slot = jnp.int32(0)
                for earlier in range(b):
                    for other in range(2):
                        slot = slot + (named[earlier][other] == named[b][j]).astype(jnp.int32)
                code[b].append(2 * named[b][j] + slot)
        return named, code

    def set_picker(s, ids):
        _, code = codes(s, ids)
        row = lax.broadcasted_iota(jnp.int32, (half, rows), 0)
        column = lax.broadcasted_iota(jnp.int32, (half, rows), 1)
        same = (row % BR == column % BR).astype(F32)
        total = jnp.zeros((half, rows), F32)
        for j in range(2):
            wanted = jnp.zeros((half, rows), jnp.int32)
            for b in range(blocks):
                wanted = wanted + (column // BR == b).astype(jnp.int32) * code[b][j]
            total = total + (row // BR == wanted).astype(F32)
        picker[s] = (total * same).astype(BF16)

    def pick(s, k):
        source = normed if s < 2 else far_normed
        chosen = jnp.dot(picker[s], source[s % 2, k], preferred_element_type=F32)
        sending[s, k] = chosen.astype(BF16)
        own = pl.ds(pl.multiple_of(x * pick_rows, pick_rows), pick_rows)
        mine = pl.ds(pl.multiple_of(own_half + x * pick_rows, pick_rows), pick_rows)
        arrived[s, k, mine, :] = sending[s, k, own, :]
        for i in range(1, XN):
            x_forward(s, k, i).start()

    def relay(s, k):
        z_forward(s % 2, k).wait_recv()
        pick(s, k)

    def gates(s, ids):
        source = normed if s < 2 else far_normed
        mb = s % 2

        @pl.loop(0, blocks)
        def _(b):
            at = pl.ds(pl.multiple_of(b * BR, BR), BR)
            sums = [jnp.zeros((BR, LANES), F32) for _ in range(EXPERTS)]
            for k in range(CHUNKS):
                for t in range(tiles):
                    value = source[mb, k, at, t * LANES : (t + 1) * LANES].astype(F32)
                    first = k * width + t * LANES
                    for e in range(EXPERTS):
                        sums[e] = sums[e] + value * router_ref[e : e + 1, first : first + LANES]
            for e in range(EXPERTS):
                total = jnp.sum(sums[e], axis=-1, keepdims=True)
                scores[e, at, :] = jnp.broadcast_to(jax.nn.sigmoid(total), (BR, LANES))

        named, code = codes(s, ids)
        column = lax.broadcasted_iota(jnp.int32, (BR, LANES), 1)
        row = lax.broadcasted_iota(jnp.int32, (BR, LANES), 0)
        same = (column % BR == row).astype(F32)
        for b in range(blocks):
            at = slice(b * BR, (b + 1) * BR)
            score = []
            for j in range(2):
                value = jnp.zeros((BR, LANES), F32)
                for e in range(EXPERTS):
                    value = value + scores[e, at, :] * (named[b][j] == e).astype(F32)
                score.append(value)
            total = score[0] + score[1]
            for first in range(0, half, LANES):
                place = (column + first) // BR
                value = jnp.zeros((BR, LANES), F32)
                for j in range(2):
                    value = value + (place == code[b][j]).astype(F32) * same * (score[j] / total)
                main = value.astype(BF16)
                mixer[s, at, first : first + LANES] = main
                mixer_rest[s, at, first : first + LANES] = (value - main.astype(F32)).astype(BF16)

    def to_core(s, k):
        for i in range(1, XN):
            x_forward(s, k, i).wait_recv()
        core_forward(s, k).start()

    def experts(s):
        for k in range(CHUNKS):
            core_forward(s, k).wait_recv()
            core_forward(s, k).wait_send()

        @pl.loop(0, 2)
        def _(t):
            at = pl.ds(pl.multiple_of(t * half, half), half)
            gate_pre = jnp.zeros((half, units), F32)
            up_pre = jnp.zeros((half, units), F32)
            for k in range(CHUNKS):
                value = arrived[s, k, at, :]
                cut = slice(k * width, (k + 1) * width)
                gate_pre = gate_pre + jnp.dot(value, gate_w[cut, :], preferred_element_type=F32)
                up_pre = up_pre + jnp.dot(value, up_w[cut, :], preferred_element_type=F32)
            hidden[at, :] = (jax.nn.silu(gate_pre) * up_pre).astype(BF16)

        @pl.loop(0, CHUNKS)
        def _(k):
            for first in (mate_half, own_half):
                at = pl.ds(first, half)
                part = jnp.dot(hidden[at, :], down_w[k], preferred_element_type=F32)
                arrived[s, k, at, :] = part.astype(BF16)
                if first is mate_half:
                    core_part(s, k).start()

    def pair_sum(s, k):
        core_part(s, k).wait_recv()

        @pl.loop(0, XN)
        def _(i):
            at = pl.ds(pl.multiple_of(i * pick_rows, pick_rows), pick_rows)
            mine = pl.ds(pl.multiple_of(own_half + i * pick_rows, pick_rows), pick_rows)
            total = arrived[s, k, mine, :].astype(F32) + core_sum[s, k, at, :].astype(F32)
            arrived[s, k, mine, :] = total.astype(BF16)

        here = pl.ds(pl.multiple_of(x * pick_rows, pick_rows), pick_rows)
        mine = pl.ds(pl.multiple_of(own_half + x * pick_rows, pick_rows), pick_rows)
        returned[s, k, here, :] = arrived[s, k, mine, :]

    def send_back(s, k):
        for i in range(1, XN):
            x_return(s, k, i).start()

    def weighted(s, k):
        value = returned[s, k]
        return jnp.dot(mixer[s], value, preferred_element_type=F32) + jnp.dot(
            mixer_rest[s], value, preferred_element_type=F32
        )

    def combine(s, k):
        mb = s % 2
        for i in range(1, XN):
            x_return(s, k, i).wait_recv()
        z_out[mb, k] = weighted(s, k).astype(BF16)
        z_return(mb, k).start()

    def finish(mb, k):
        for i in range(1, XN):
            x_return(mb, k, i).wait_recv()
        z_return(mb, k).wait_recv()
        total = weighted(mb, k) + z_in[mb, k].astype(F32)
        mixed = acts[mb, :, k * width : (k + 1) * width].astype(F32) + ROUTE_SCALE * total
        finished[mb, k] = mixed.astype(BF16)
        if k < len(DETOURS[mb]):

            @pl.when(at_edge[mb])
            def _():
                detour(mb, k).start()

            @pl.when(jnp.logical_not(at_edge[mb]))
            def _():
                shift(mb, k).start()

        else:
            shift(mb, k).start()

    def pass_on(mb, k):
        if k >= len(DETOURS[mb]):
            return

        @pl.when(y == DETOURS[mb][k])
        def _():
            detour(mb, k).wait_recv()
            onward(mb, k).start()

    act_copies = [
        pltpu.make_async_copy(source.at[0], acts.at[mb], act_sem.at[mb])
        for mb, source in enumerate((rise_hbm, fall_hbm))
    ]
    weight_copies = [
        pltpu.make_async_copy(gate_hbm.at[0], gate_w, w_sem.at[0]),
        pltpu.make_async_copy(up_hbm.at[0], up_w, w_sem.at[1]),
    ] + [
        pltpu.make_async_copy(down_hbm.at[0, :, pl.ds(k * width, width)], down_w.at[k], dw_sem.at[k])
        for k in range(CHUNKS)
    ]
    ids_copy = pltpu.make_async_copy(ids_hbm, ids_own, ids_sem.at[0])
    act_copies[0].start()
    ids_copy.start()
    act_copies[1].start()

    barrier = pltpu.get_barrier_semaphore()
    partners = [(seg, x_device(i)) for i in range(1, XN)]
    partners += [(seg, z_mate), (seg, core_mate), (base_up, me), (base_down + YN - 1, me)]
    partners += [(seg_base + lax.rem(y + j, YN), me) for j in range(1, YN)]

    def greet(partner):
        pl.semaphore_signal(barrier, inc=1, device_id=partner, device_id_type=MESH)

    for partner in partners:
        greet(partner)

    @pl.when(at_edge[1])
    def _():
        for j in range(YN - 1):
            greet((base_down + j, me))

    @pl.when(at_edge[0])
    def _():
        for j in range(1, YN):
            greet((base_up + j, me))

    at_either = jnp.logical_or(at_edge[0], at_edge[1]).astype(jnp.int32)

    act_copies[0].wait()
    normalize(0)
    for copy in weight_copies:
        copy.start()
    ids_copy.wait()
    set_picker(0, ids_own)
    pl.semaphore_wait(barrier, len(partners) + (YN - 1) * at_either)

    every = range(CHUNKS)
    rise, fall, far_rise, far_fall = range(4)
    ids_exchange.start()
    for k in every:
        z_forward(0, k).start()
    for k in every:
        pick(rise, k)
    set_picker(fall, ids_own)
    act_copies[1].wait()
    normalize(1)
    for k in every:
        z_forward(1, k).start()
    gates(rise, ids_own)
    ids_exchange.wait()
    ids_far_copy = pltpu.make_async_copy(ids_land, ids_far, ids_sem.at[1])
    ids_far_copy.start()
    ids_far_copy.wait()
    set_picker(far_rise, ids_far)
    set_picker(far_fall, ids_far)
    to_core(rise, 0)
    relay(far_rise, 0)
    pick(fall, 0)
    for k in every[1:]:
        to_core(rise, k)
    for copy in weight_copies:
        copy.wait()
    pick(fall, 1)
    experts(rise)
    for k in every[1:]:
        relay(far_rise, k)
        if k + 1 < CHUNKS:
            pick(fall, k + 1)
    for k in every:
        pair_sum(rise, k)
    gates(fall, ids_own)
    for k in every:
        to_core(far_rise, k)
        to_core(fall, k)
    for k in every[: FILL[0]]:
        send_back(rise, k)
    experts(far_rise)
    for k in every:
        pair_sum(far_rise, k)
        send_back(far_rise, k)
    gates(far_rise, ids_far)
    for k in every[: CHUNKS // 2]:
        relay(far_fall, k)
    experts(fall)
    for k in every:
        pair_sum(fall, k)
    for k in every[: CHUNKS // 2]:
        combine(far_rise, k)
    for k in every[CHUNKS // 2 :]:
        relay(far_fall, k)
        combine(far_rise, k)
    gates(far_fall, ids_far)
    for k in every[FILL[0] : FILL[1]]:
        send_back(rise, k)
    for k in every:
        to_core(far_fall, k)
    experts(far_fall)
    for k in every:
        pair_sum(far_fall, k)
        send_back(far_fall, k)
    for k in every[FILL[1] :]:
        send_back(rise, k)
    for k in every:
        send_back(fall, k)
    early = max(FILL[1] - 1, 1)
    for k in every[:early]:
        finish(0, k)
    for k in every:
        combine(far_fall, k)
        if k < early:
            pass_on(0, k)
    last = [(0, k) for k in every[early:]] + [(1, k) for k in every]
    for i, step in enumerate(last):
        finish(*step)
        if i >= 2:
            pass_on(*last[i - 2])
    for step in last[-2:]:
        pass_on(*step)

    for k in every:
        for mb in range(2):
            z_forward(mb, k).wait_send()
            z_return(mb, k).wait_send()
            shift(mb, k).wait_send()
        for s in range(4):
            core_part(s, k).wait_send()
            for i in range(1, XN):
                x_forward(s, k, i).wait_send()
                x_return(s, k, i).wait_send()
    for mb in range(2):
        for k, by in enumerate(DETOURS[mb]):

            @pl.when(y == by)
            def _():
                onward(mb, k).wait_send()

    for k in every:
        for mb in range(2):
            shift(mb, k).wait_recv()


def on_device(
    rising_acts,
    falling_acts,
    norm_gain,
    router_weight,
    gate_weight,
    up_weight,
    down_weight,
    rising_ids,
    falling_ids,
):
    rows, features = rising_acts.shape[1:]
    units = gate_weight.shape[2]
    width = features // CHUNKS
    half = XN * 2 * BR
    segments = lax.axis_size("segment")
    named = jnp.concatenate([rising_ids[0].T, falling_ids[0].T], axis=0)
    ids = jnp.pad(named, ((0, 8 - named.shape[0]), (0, LANES - named.shape[1])))
    dma = pltpu.SemaphoreType.DMA
    hbm = pl.BlockSpec(memory_space=pl.ANY)
    vmem = pl.BlockSpec(memory_space=pltpu.VMEM)
    result = jax.ShapeDtypeStruct(rising_acts.shape, BF16)
    return pl.pallas_call(
        functools.partial(relay_kernel, rows, features, units, segments),
        out_shape=(result, result),
        in_specs=[hbm, hbm, vmem, vmem, hbm, hbm, hbm, hbm],
        out_specs=(hbm, hbm),
        scratch_shapes=[
            pltpu.VMEM((2, rows, features), BF16),
            pltpu.VMEM((features, units), BF16),
            pltpu.VMEM((features, units), BF16),
            pltpu.VMEM((CHUNKS, units, width), BF16),
            pltpu.SMEM((8, LANES), jnp.int32),
            pltpu.VMEM((8, LANES), jnp.int32),
            pltpu.SMEM((8, LANES), jnp.int32),
            pltpu.VMEM((4, half, rows), BF16),
            pltpu.VMEM((4, rows, half), BF16),
            pltpu.VMEM((4, rows, half), BF16),
            pltpu.VMEM((2, CHUNKS, rows, width), BF16),
            pltpu.VMEM((2, CHUNKS, rows, width), BF16),
            pltpu.VMEM((4, CHUNKS, half, width), BF16),
            pltpu.VMEM((4, CHUNKS, 2 * half, width), BF16),
            pltpu.VMEM((2 * half, units), BF16),
            pltpu.VMEM((4, CHUNKS, half, width), BF16),
            pltpu.VMEM((4, CHUNKS, half, width), BF16),
            pltpu.VMEM((2, CHUNKS, rows, width), BF16),
            pltpu.VMEM((2, CHUNKS, rows, width), BF16),
            pltpu.VMEM((2, CHUNKS, rows, width), BF16),
            pltpu.VMEM((EXPERTS, rows, LANES), F32),
            dma((2,)),
            dma((2,)),
            dma((CHUNKS,)),
            dma((2,)),
            dma,
            dma,
            dma((2, CHUNKS)),
            dma((2, CHUNKS)),
            dma((4, CHUNKS, XN - 1)),
            dma((4, CHUNKS, XN - 1)),
            dma((4, CHUNKS)),
            dma((4, CHUNKS)),
            dma((4, CHUNKS)),
            dma((4, CHUNKS)),
            dma((4, CHUNKS, XN - 1)),
            dma((4, CHUNKS, XN - 1)),
            dma((2, CHUNKS)),
            dma((2, CHUNKS)),
            dma((2, CHUNKS)),
            dma((2, CHUNKS)),
            pltpu.VMEM((2, len(DETOURS[0]), rows, width), BF16),
            dma((2, CHUNKS)),
            dma((2, CHUNKS)),
        ],
        compiler_params=pltpu.CompilerParams(
            collective_id=0, has_side_effects=True, vmem_limit_bytes=60 << 20
        ),
        name="relay",
    )(
        rising_acts,
        falling_acts,
        norm_gain,
        router_weight[0].T,
        gate_weight,
        up_weight,
        down_weight,
        ids,
    )


def solution(mesh):
    return jax.shard_map(
        on_device,
        mesh=mesh,
        in_specs=(
            P("segment", "expert", None),
            P("segment", "expert", None),
            P("segment", None),
            P("segment", None, None),
            P("segment", None, "expert"),
            P("segment", None, "expert"),
            P("segment", "expert", None),
            P("segment", "expert", None),
            P("segment", "expert", None),
        ),
        out_specs=(P("segment", "expert", None), P("segment", "expert", None)),
        check_vma=False,
    )
```

```python
import functools

import jax
import jax.numpy as jnp
from jax import lax
from jax.experimental import pallas as pl
from jax.experimental.pallas import tpu as pltpu
from jax.sharding import PartitionSpec as P

MESH = pl.DeviceIdType.MESH
EPS = 1e-06
ROUTE_SCALE = 2.5
EXPERTS = 4
XN = 4
CHUNKS = 7
FILL = (2, 5)
YN = 4
DETOURS = ((1, 2, 0, 1, 2), (2, 1, 3, 2))
BR = 32
LANES = 128
F32 = jnp.float32
BF16 = jnp.bfloat16


def relay_kernel(
    rows,
    features,
    units,
    segments,
    rise_hbm,
    fall_hbm,
    gain_ref,
    router_ref,
    gate_hbm,
    up_hbm,
    down_hbm,
    rise_ids,
    fall_ids,
    rise_out,
    fall_out,
    acts,
    gate_w,
    up_w,
    down_w,
    ids_land,
    ids_rise,
    ids_fall,
    far_rise_ids,
    far_fall_ids,
    picker,
    mixer,
    mixer_rest,
    normed,
    far_normed,
    sending,
    arrived,
    hidden,
    core_sum,
    returned,
    z_out,
    z_in,
    finished,
    scores,
    act_sem,
    w_sem,
    dw_sem,
    ids_sem,
    ids_ss,
    ids_rs,
    zf_ss,
    zf_rs,
    xf_ss,
    xf_rs,
    df_ss,
    df_rs,
    dp_ss,
    dp_rs,
    xr_ss,
    xr_rs,
    zr_ss,
    zr_rs,
    y_ss,
    y_rs,
    passing,
    pass_ss,
    pass_rs,
):
    width = features // CHUNKS
    pick_rows = 2 * BR
    half = XN * pick_rows
    blocks = rows // BR
    tiles = width // LANES

    seg = lax.axis_index("segment")
    me = lax.axis_index("expert")
    x = me // 4
    core = lax.rem(me, 2)
    z_hi = lax.rem(me // 2, 2)
    z_mate = me + 2 - 4 * z_hi
    core_mate = me + 1 - 2 * core
    seg_up = lax.rem(seg + 1, segments)
    seg_down = lax.rem(seg + segments - 1, segments)
    y = lax.rem(seg, YN)
    z_lo = seg // YN
    z_count = segments // YN
    seg_base = seg - y
    base_up = lax.rem(z_lo + 1, z_count) * YN
    base_down = lax.rem(z_lo + z_count - 1, z_count) * YN
    at_edge = (y == YN - 1, y == 0)
    past_edge = (base_up, base_down + YN - 1)
    own_half = pl.multiple_of(core * half, half)
    mate_half = pl.multiple_of((1 - core) * half, half)

    def x_at(i):
        return lax.rem(x + i, XN)

    def x_device(i):
        return me + 4 * (x_at(i) - x)

    def z_forward(mb, k):
        return pltpu.make_async_remote_copy(
            src_ref=normed.at[mb, k],
            dst_ref=far_normed.at[mb, k],
            send_sem=zf_ss.at[mb, k],
            recv_sem=zf_rs.at[mb, k],
            device_id=(seg, z_mate),
            device_id_type=MESH,
        )

    def x_forward(s, k, i):
        return pltpu.make_async_remote_copy(
            src_ref=sending.at[s, k, pl.ds(pl.multiple_of(x_at(i) * pick_rows, pick_rows), pick_rows)],
            dst_ref=arrived.at[s, k, pl.ds(pl.multiple_of(own_half + x * pick_rows, pick_rows), pick_rows)],
            send_sem=xf_ss.at[s, k, i - 1],
            recv_sem=xf_rs.at[s, k, i - 1],
            device_id=(seg, x_device(i)),
            device_id_type=MESH,
        )

    def core_forward(s, k):
        return pltpu.make_async_remote_copy(
            src_ref=arrived.at[s, k, pl.ds(own_half, half)],
            dst_ref=arrived.at[s, k, pl.ds(own_half, half)],
            send_sem=df_ss.at[s, k],
            recv_sem=df_rs.at[s, k],
            device_id=(seg, core_mate),
            device_id_type=MESH,
        )

    def core_part(s, k):
        return pltpu.make_async_remote_copy(
            src_ref=arrived.at[s, k, pl.ds(mate_half, half)],
            dst_ref=core_sum.at[s, k],
            send_sem=dp_ss.at[s, k],
            recv_sem=dp_rs.at[s, k],
            device_id=(seg, core_mate),
            device_id_type=MESH,
        )

    def x_return(s, k, i):
        return pltpu.make_async_remote_copy(
            src_ref=arrived.at[s, k, pl.ds(pl.multiple_of(own_half + x_at(i) * pick_rows, pick_rows), pick_rows)],
            dst_ref=returned.at[s, k, pl.ds(pl.multiple_of(x * pick_rows, pick_rows), pick_rows)],
            send_sem=xr_ss.at[s, k, i - 1],
            recv_sem=xr_rs.at[s, k, i - 1],
            device_id=(seg, x_device(i)),
            device_id_type=MESH,
        )

    def z_return(mb, k):
        return pltpu.make_async_remote_copy(
            src_ref=z_out.at[mb, k],
            dst_ref=z_in.at[mb, k],
            send_sem=zr_ss.at[mb, k],
            recv_sem=zr_rs.at[mb, k],
            device_id=(seg, z_mate),
            device_id_type=MESH,
        )

    def shift(mb, k):
        out = rise_out if mb == 0 else fall_out
        return pltpu.make_async_remote_copy(
            src_ref=finished.at[mb, k],
            dst_ref=out.at[0, :, pl.ds(k * width, width)],
            send_sem=y_ss.at[mb, k],
            recv_sem=y_rs.at[mb, k],
            device_id=(seg_up if mb == 0 else seg_down, me),
            device_id_type=MESH,
        )

    def detour(mb, k):
        return pltpu.make_async_remote_copy(
            src_ref=finished.at[mb, k],
            dst_ref=passing.at[mb, k],
            send_sem=y_ss.at[mb, k],
            recv_sem=pass_rs.at[mb, k],
            device_id=(seg_base + DETOURS[mb][k], me),
            device_id_type=MESH,
        )

    def onward(mb, k):
        out = rise_out if mb == 0 else fall_out
        return pltpu.make_async_remote_copy(
            src_ref=passing.at[mb, k],
            dst_ref=out.at[0, :, pl.ds(k * width, width)],
            send_sem=pass_ss.at[mb, k],
            recv_sem=y_rs.at[mb, k],
            device_id=(past_edge[mb], me),
            device_id_type=MESH,
        )

    ids_exchange = [
        pltpu.make_async_remote_copy(
            src_ref=source,
            dst_ref=ids_land.at[mb],
            send_sem=ids_ss.at[mb],
            recv_sem=ids_rs.at[mb],
            device_id=(seg, z_mate),
            device_id_type=MESH,
        )
        for mb, source in enumerate((rise_ids, fall_ids))
    ]

    def normalize(mb):
        @pl.loop(0, blocks)
        def _(b):
            at = pl.ds(pl.multiple_of(b * BR, BR), BR)
            value = acts[mb, at, :].astype(F32)
            scale = lax.rsqrt(jnp.mean(value * value, axis=-1, keepdims=True) + EPS)
            for k in range(CHUNKS):
                cut = slice(k * width, (k + 1) * width)
                normed[mb, k, at, :] = (value[:, cut] * scale * gain_ref[:, cut]).astype(BF16)

    def codes(s, ids):
        mb = s % 2
        named = [[ids[mb][j, b] for j in range(2)] for b in range(blocks)]
        code = []
        for b in range(blocks):
            code.append([])
            for j in range(2):
                slot = jnp.int32(0)
                for earlier in range(b):
                    for other in range(2):
                        slot = slot + (named[earlier][other] == named[b][j]).astype(jnp.int32)
                code[b].append(2 * named[b][j] + slot)
        return named, code

    def set_picker(s, ids):
        _, code = codes(s, ids)
        row = lax.broadcasted_iota(jnp.int32, (half, rows), 0)
        column = lax.broadcasted_iota(jnp.int32, (half, rows), 1)
        same = (row % BR == column % BR).astype(F32)
        total = jnp.zeros((half, rows), F32)
        for j in range(2):
            wanted = jnp.zeros((half, rows), jnp.int32)
            for b in range(blocks):
                wanted = wanted + (column // BR == b).astype(jnp.int32) * code[b][j]
            total = total + (row // BR == wanted).astype(F32)
        picker[s] = (total * same).astype(BF16)

    def pick(s, k):
        source = normed if s < 2 else far_normed
        chosen = jnp.dot(picker[s], source[s % 2, k], preferred_element_type=F32)
        sending[s, k] = chosen.astype(BF16)
        own = pl.ds(pl.multiple_of(x * pick_rows, pick_rows), pick_rows)
        mine = pl.ds(pl.multiple_of(own_half + x * pick_rows, pick_rows), pick_rows)
        arrived[s, k, mine, :] = sending[s, k, own, :]
        for i in range(1, XN):
            x_forward(s, k, i).start()

    def relay(s, k):
        z_forward(s % 2, k).wait_recv()
        pick(s, k)

    def gates(s, ids):
        source = normed if s < 2 else far_normed
        mb = s % 2

        @pl.loop(0, blocks)
        def _(b):
            at = pl.ds(pl.multiple_of(b * BR, BR), BR)
            sums = [jnp.zeros((BR, LANES), F32) for _ in range(EXPERTS)]
            for k in range(CHUNKS):
                for t in range(tiles):
                    value = source[mb, k, at, t * LANES : (t + 1) * LANES].astype(F32)
                    first = k * width + t * LANES
                    for e in range(EXPERTS):
                        sums[e] = sums[e] + value * router_ref[e : e + 1, first : first + LANES]
            for e in range(EXPERTS):
                total = jnp.sum(sums[e], axis=-1, keepdims=True)
                scores[e, at, :] = jnp.broadcast_to(jax.nn.sigmoid(total), (BR, LANES))

        named, code = codes(s, ids)
        column = lax.broadcasted_iota(jnp.int32, (BR, LANES), 1)
        row = lax.broadcasted_iota(jnp.int32, (BR, LANES), 0)
        same = (column % BR == row).astype(F32)
        for b in range(blocks):
            at = slice(b * BR, (b + 1) * BR)
            score = []
            for j in range(2):
                value = jnp.zeros((BR, LANES), F32)
                for e in range(EXPERTS):
                    value = value + scores[e, at, :] * (named[b][j] == e).astype(F32)
                score.append(value)
            total = score[0] + score[1]
            for first in range(0, half, LANES):
                place = (column + first) // BR
                value = jnp.zeros((BR, LANES), F32)
                for j in range(2):
                    value = value + (place == code[b][j]).astype(F32) * same * (score[j] / total)
                main = value.astype(BF16)
                mixer[s, at, first : first + LANES] = main
                mixer_rest[s, at, first : first + LANES] = (value - main.astype(F32)).astype(BF16)

    def to_core(s, k):
        for i in range(1, XN):
            x_forward(s, k, i).wait_recv()
        core_forward(s, k).start()

    def experts(s):
        for k in range(CHUNKS):
            core_forward(s, k).wait_recv()
            core_forward(s, k).wait_send()

        @pl.loop(0, 2)
        def _(t):
            at = pl.ds(pl.multiple_of(t * half, half), half)
            gate_pre = jnp.zeros((half, units), F32)
            up_pre = jnp.zeros((half, units), F32)
            for k in range(CHUNKS):
                value = arrived[s, k, at, :]
                cut = slice(k * width, (k + 1) * width)
                gate_pre = gate_pre + jnp.dot(value, gate_w[cut, :], preferred_element_type=F32)
                up_pre = up_pre + jnp.dot(value, up_w[cut, :], preferred_element_type=F32)
            hidden[at, :] = (jax.nn.silu(gate_pre) * up_pre).astype(BF16)

        @pl.loop(0, CHUNKS)
        def _(k):
            for first in (mate_half, own_half):
                at = pl.ds(first, half)
                part = jnp.dot(hidden[at, :], down_w[k], preferred_element_type=F32)
                arrived[s, k, at, :] = part.astype(BF16)
                if first is mate_half:
                    core_part(s, k).start()

    def pair_sum(s, k):
        core_part(s, k).wait_recv()

        @pl.loop(0, XN)
        def _(i):
            at = pl.ds(pl.multiple_of(i * pick_rows, pick_rows), pick_rows)
            mine = pl.ds(pl.multiple_of(own_half + i * pick_rows, pick_rows), pick_rows)
            total = arrived[s, k, mine, :].astype(F32) + core_sum[s, k, at, :].astype(F32)
            arrived[s, k, mine, :] = total.astype(BF16)

        here = pl.ds(pl.multiple_of(x * pick_rows, pick_rows), pick_rows)
        mine = pl.ds(pl.multiple_of(own_half + x * pick_rows, pick_rows), pick_rows)
        returned[s, k, here, :] = arrived[s, k, mine, :]

    def send_back(s, k):
        for i in range(1, XN):
            x_return(s, k, i).start()

    def weighted(s, k):
        value = returned[s, k]
        return jnp.dot(mixer[s], value, preferred_element_type=F32) + jnp.dot(
            mixer_rest[s], value, preferred_element_type=F32
        )

    def combine(s, k):
        mb = s % 2
        for i in range(1, XN):
            x_return(s, k, i).wait_recv()
        z_out[mb, k] = weighted(s, k).astype(BF16)
        z_return(mb, k).start()

    def finish(mb, k):
        for i in range(1, XN):
            x_return(mb, k, i).wait_recv()
        z_return(mb, k).wait_recv()
        total = weighted(mb, k) + z_in[mb, k].astype(F32)
        mixed = acts[mb, :, k * width : (k + 1) * width].astype(F32) + ROUTE_SCALE * total
        finished[mb, k] = mixed.astype(BF16)
        if k < len(DETOURS[mb]):

            @pl.when(at_edge[mb])
            def _():
                detour(mb, k).start()

            @pl.when(jnp.logical_not(at_edge[mb]))
            def _():
                shift(mb, k).start()

        else:
            shift(mb, k).start()

    def pass_on(mb, k):
        if k >= len(DETOURS[mb]):
            return

        @pl.when(y == DETOURS[mb][k])
        def _():
            detour(mb, k).wait_recv()
            onward(mb, k).start()

    act_copies = [
        pltpu.make_async_copy(source.at[0], acts.at[mb], act_sem.at[mb])
        for mb, source in enumerate((rise_hbm, fall_hbm))
    ]
    weight_copies = [
        pltpu.make_async_copy(gate_hbm.at[0], gate_w, w_sem.at[0]),
        pltpu.make_async_copy(up_hbm.at[0], up_w, w_sem.at[1]),
    ] + [
        pltpu.make_async_copy(down_hbm.at[0, :, pl.ds(k * width, width)], down_w.at[k], dw_sem.at[k])
        for k in range(CHUNKS)
    ]
    ids_own = (ids_rise, ids_fall)
    ids_far = (far_rise_ids, far_fall_ids)
    ids_copies = [
        pltpu.make_async_copy(source, ids_own[mb], ids_sem.at[mb])
        for mb, source in enumerate((rise_ids, fall_ids))
    ]
    ids_far_copies = [
        pltpu.make_async_copy(ids_land.at[mb], ids_far[mb], ids_sem.at[2 + mb]) for mb in range(2)
    ]
    act_copies[0].start()
    for copy in ids_copies:
        copy.start()
    act_copies[1].start()

    barrier = pltpu.get_barrier_semaphore()
    partners = [(seg, x_device(i)) for i in range(1, XN)]
    partners += [(seg, z_mate), (seg, core_mate), (base_up, me), (base_down + YN - 1, me)]
    partners += [(seg_base + lax.rem(y + j, YN), me) for j in range(1, YN)]

    def greet(partner):
        pl.semaphore_signal(barrier, inc=1, device_id=partner, device_id_type=MESH)

    for partner in partners:
        greet(partner)

    @pl.when(at_edge[1])
    def _():
        for j in range(YN - 1):
            greet((base_down + j, me))

    @pl.when(at_edge[0])
    def _():
        for j in range(1, YN):
            greet((base_up + j, me))

    at_either = jnp.logical_or(at_edge[0], at_edge[1]).astype(jnp.int32)

    act_copies[0].wait()
    normalize(0)
    for copy in weight_copies:
        copy.start()
    for copy in ids_copies:
        copy.wait()
    set_picker(0, ids_own)
    pl.semaphore_wait(barrier, len(partners) + (YN - 1) * at_either)

    every = range(CHUNKS)
    rise, fall, far_rise, far_fall = range(4)
    for copy in ids_exchange:
        copy.start()
    for k in every:
        z_forward(0, k).start()
    for k in every:
        pick(rise, k)
    set_picker(fall, ids_own)
    act_copies[1].wait()
    normalize(1)
    for k in every:
        z_forward(1, k).start()
    gates(rise, ids_own)
    for copy in ids_exchange:
        copy.wait()
    for copy in ids_far_copies:
        copy.start()
    for copy in ids_far_copies:
        copy.wait()
    set_picker(far_rise, ids_far)
    set_picker(far_fall, ids_far)
    to_core(rise, 0)
    relay(far_rise, 0)
    pick(fall, 0)
    for k in every[1:]:
        to_core(rise, k)
    for copy in weight_copies:
        copy.wait()
    pick(fall, 1)
    experts(rise)
    for k in every[1:]:
        relay(far_rise, k)
        if k + 1 < CHUNKS:
            pick(fall, k + 1)
    for k in every:
        pair_sum(rise, k)
    gates(fall, ids_own)
    for k in every:
        to_core(far_rise, k)
        to_core(fall, k)
    for k in every[: FILL[0]]:
        send_back(rise, k)
    experts(far_rise)
    for k in every:
        pair_sum(far_rise, k)
        send_back(far_rise, k)
    gates(far_rise, ids_far)
    for k in every[: CHUNKS // 2]:
        relay(far_fall, k)
    experts(fall)
    for k in every:
        pair_sum(fall, k)
    for k in every[: CHUNKS // 2]:
        combine(far_rise, k)
    for k in every[CHUNKS // 2 :]:
        relay(far_fall, k)
        combine(far_rise, k)
    gates(far_fall, ids_far)
    for k in every[FILL[0] : FILL[1]]:
        send_back(rise, k)
    for k in every:
        to_core(far_fall, k)
        if 1 <= k <= FILL[0]:
            finish(0, k - 1)
    for k in every[: FILL[0]]:
        pass_on(0, k)
    experts(far_fall)
    for k in every:
        pair_sum(far_fall, k)
        send_back(far_fall, k)
    late = list(every[FILL[1] :])
    for k in every:
        send_back(fall, k)
        if k < len(late):
            send_back(rise, late[k])
    for k in every[FILL[0] : FILL[1]]:
        finish(0, k)
    for k in every:
        combine(far_fall, k)
        if FILL[0] <= k < FILL[1]:
            pass_on(0, k)
    last = []
    for k in every:
        last.append((1, k))
        if k < len(late):
            last.append((0, late[k]))
    waiting = []
    for mb, k in last:
        finish(mb, k)
        while waiting and waiting[0][2] <= 1:
            pass_on(*waiting.pop(0)[:2])
        waiting = [(*step, lag - 1) for *step, lag in waiting]
        waiting.append((mb, k, 1 if mb == 1 and k >= 2 else 2))
    for mb, k, _ in waiting:
        pass_on(mb, k)

    for k in every:
        for mb in range(2):
            z_forward(mb, k).wait_send()
            z_return(mb, k).wait_send()
            shift(mb, k).wait_send()
        for s in range(4):
            core_part(s, k).wait_send()
            for i in range(1, XN):
                x_forward(s, k, i).wait_send()
                x_return(s, k, i).wait_send()
    for mb in range(2):
        for k, by in enumerate(DETOURS[mb]):

            @pl.when(y == by)
            def _():
                onward(mb, k).wait_send()

    for k in every:
        for mb in range(2):
            shift(mb, k).wait_recv()


def on_device(
    rising_acts,
    falling_acts,
    norm_gain,
    router_weight,
    gate_weight,
    up_weight,
    down_weight,
    rising_ids,
    falling_ids,
):
    rows, features = rising_acts.shape[1:]
    units = gate_weight.shape[2]
    width = features // CHUNKS
    half = XN * 2 * BR
    segments = lax.axis_size("segment")
    top, blocks = rising_ids.shape[2], rising_ids.shape[1]
    dma = pltpu.SemaphoreType.DMA
    hbm = pl.BlockSpec(memory_space=pl.ANY)
    vmem = pl.BlockSpec(memory_space=pltpu.VMEM)
    result = jax.ShapeDtypeStruct(rising_acts.shape, BF16)
    return pl.pallas_call(
        functools.partial(relay_kernel, rows, features, units, segments),
        out_shape=(result, result),
        in_specs=[hbm, hbm, vmem, vmem, hbm, hbm, hbm, hbm, hbm],
        out_specs=(hbm, hbm),
        scratch_shapes=[
            pltpu.VMEM((2, rows, features), BF16),
            pltpu.VMEM((features, units), BF16),
            pltpu.VMEM((features, units), BF16),
            pltpu.VMEM((CHUNKS, units, width), BF16),
            pltpu.VMEM((2, top, blocks), jnp.int32),
        ]
        + [pltpu.SMEM((top, blocks), jnp.int32)] * 4
        + [
            pltpu.VMEM((4, half, rows), BF16),
            pltpu.VMEM((4, rows, half), BF16),
            pltpu.VMEM((4, rows, half), BF16),
            pltpu.VMEM((2, CHUNKS, rows, width), BF16),
            pltpu.VMEM((2, CHUNKS, rows, width), BF16),
            pltpu.VMEM((4, CHUNKS, half, width), BF16),
            pltpu.VMEM((4, CHUNKS, 2 * half, width), BF16),
            pltpu.VMEM((2 * half, units), BF16),
            pltpu.VMEM((4, CHUNKS, half, width), BF16),
            pltpu.VMEM((4, CHUNKS, half, width), BF16),
            pltpu.VMEM((2, CHUNKS, rows, width), BF16),
            pltpu.VMEM((2, CHUNKS, rows, width), BF16),
            pltpu.VMEM((2, CHUNKS, rows, width), BF16),
            pltpu.VMEM((EXPERTS, rows, LANES), F32),
            dma((2,)),
            dma((2,)),
            dma((CHUNKS,)),
            dma((4,)),
            dma((2,)),
            dma((2,)),
            dma((2, CHUNKS)),
            dma((2, CHUNKS)),
            dma((4, CHUNKS, XN - 1)),
            dma((4, CHUNKS, XN - 1)),
            dma((4, CHUNKS)),
            dma((4, CHUNKS)),
            dma((4, CHUNKS)),
            dma((4, CHUNKS)),
            dma((4, CHUNKS, XN - 1)),
            dma((4, CHUNKS, XN - 1)),
            dma((2, CHUNKS)),
            dma((2, CHUNKS)),
            dma((2, CHUNKS)),
            dma((2, CHUNKS)),
            pltpu.VMEM((2, len(DETOURS[0]), rows, width), BF16),
            dma((2, CHUNKS)),
            dma((2, CHUNKS)),
        ],
        compiler_params=pltpu.CompilerParams(
            collective_id=0, has_side_effects=True, vmem_limit_bytes=60 << 20
        ),
        name="relay",
    )(
        rising_acts,
        falling_acts,
        norm_gain,
        router_weight[0].T,
        gate_weight,
        up_weight,
        down_weight,
        rising_ids[0].T,
        falling_ids[0].T,
    )


def solution(mesh):
    return jax.shard_map(
        on_device,
        mesh=mesh,
        in_specs=(
            P("segment", "expert", None),
            P("segment", "expert", None),
            P("segment", None),
            P("segment", None, None),
            P("segment", None, "expert"),
            P("segment", None, "expert"),
            P("segment", "expert", None),
            P("segment", "expert", None),
            P("segment", "expert", None),
        ),
        out_specs=(P("segment", "expert", None), P("segment", "expert", None)),
        check_vma=False,
    )
```

```python
import functools

import jax
import jax.numpy as jnp
from jax import lax
from jax.experimental import pallas as pl
from jax.experimental.pallas import tpu as pltpu
from jax.sharding import PartitionSpec as P

MESH = pl.DeviceIdType.MESH
EPS = 1e-06
ROUTE_SCALE = 2.5
EXPERTS = 4
XN = 4
FAR_FIRST = (2, 1, 3)
CHUNKS = 7
FILL = (2, 5)
YN = 4
DETOURS = ((1, 2, 0, 1, 2), (2, 1, 3, 2))
BR = 32
LANES = 128
F32 = jnp.float32
BF16 = jnp.bfloat16


def relay_kernel(
    rows,
    features,
    units,
    segments,
    rise_hbm,
    fall_hbm,
    gain_ref,
    router_ref,
    gate_hbm,
    up_hbm,
    down_hbm,
    rise_ids,
    fall_ids,
    rise_out,
    fall_out,
    acts,
    gate_w,
    up_w,
    down_w,
    ids_land,
    ids_rise,
    ids_fall,
    far_rise_ids,
    far_fall_ids,
    picker,
    mixer,
    mixer_rest,
    normed,
    far_normed,
    sending,
    arrived,
    hidden,
    core_sum,
    returned,
    z_out,
    z_in,
    finished,
    scores,
    act_sem,
    w_sem,
    dw_sem,
    ids_sem,
    ids_ss,
    ids_rs,
    zf_ss,
    zf_rs,
    xf_ss,
    xf_rs,
    df_ss,
    df_rs,
    dp_ss,
    dp_rs,
    xr_ss,
    xr_rs,
    zr_ss,
    zr_rs,
    y_ss,
    y_rs,
    passing,
    pass_ss,
    pass_rs,
):
    width = features // CHUNKS
    pick_rows = 2 * BR
    half = XN * pick_rows
    blocks = rows // BR
    tiles = width // LANES

    seg = lax.axis_index("segment")
    me = lax.axis_index("expert")
    x = me // 4
    core = lax.rem(me, 2)
    z_hi = lax.rem(me // 2, 2)
    z_mate = me + 2 - 4 * z_hi
    core_mate = me + 1 - 2 * core
    seg_up = lax.rem(seg + 1, segments)
    seg_down = lax.rem(seg + segments - 1, segments)
    y = lax.rem(seg, YN)
    z_lo = seg // YN
    z_count = segments // YN
    seg_base = seg - y
    base_up = lax.rem(z_lo + 1, z_count) * YN
    base_down = lax.rem(z_lo + z_count - 1, z_count) * YN
    at_edge = (y == YN - 1, y == 0)
    past_edge = (base_up, base_down + YN - 1)
    own_half = pl.multiple_of(core * half, half)
    mate_half = pl.multiple_of((1 - core) * half, half)

    def x_at(i):
        return lax.rem(x + i, XN)

    def x_device(i):
        return me + 4 * (x_at(i) - x)

    def z_forward(mb, k):
        return pltpu.make_async_remote_copy(
            src_ref=normed.at[mb, k],
            dst_ref=far_normed.at[mb, k],
            send_sem=zf_ss.at[mb, k],
            recv_sem=zf_rs.at[mb, k],
            device_id=(seg, z_mate),
            device_id_type=MESH,
        )

    def x_forward(s, k, i):
        return pltpu.make_async_remote_copy(
            src_ref=sending.at[s, k, pl.ds(pl.multiple_of(x_at(i) * pick_rows, pick_rows), pick_rows)],
            dst_ref=arrived.at[s, k, pl.ds(pl.multiple_of(own_half + x * pick_rows, pick_rows), pick_rows)],
            send_sem=xf_ss.at[s, k, i - 1],
            recv_sem=xf_rs.at[s, k, i - 1],
            device_id=(seg, x_device(i)),
            device_id_type=MESH,
        )

    def core_forward(s, k):
        return pltpu.make_async_remote_copy(
            src_ref=arrived.at[s, k, pl.ds(own_half, half)],
            dst_ref=arrived.at[s, k, pl.ds(own_half, half)],
            send_sem=df_ss.at[s, k],
            recv_sem=df_rs.at[s, k],
            device_id=(seg, core_mate),
            device_id_type=MESH,
        )

    def core_part(s, k):
        return pltpu.make_async_remote_copy(
            src_ref=arrived.at[s, k, pl.ds(mate_half, half)],
            dst_ref=core_sum.at[s, k],
            send_sem=dp_ss.at[s, k],
            recv_sem=dp_rs.at[s, k],
            device_id=(seg, core_mate),
            device_id_type=MESH,
        )

    def x_return(s, k, i):
        return pltpu.make_async_remote_copy(
            src_ref=arrived.at[s, k, pl.ds(pl.multiple_of(own_half + x_at(i) * pick_rows, pick_rows), pick_rows)],
            dst_ref=returned.at[s, k, pl.ds(pl.multiple_of(x * pick_rows, pick_rows), pick_rows)],
            send_sem=xr_ss.at[s, k, i - 1],
            recv_sem=xr_rs.at[s, k, i - 1],
            device_id=(seg, x_device(i)),
            device_id_type=MESH,
        )

    def z_return(mb, k):
        return pltpu.make_async_remote_copy(
            src_ref=z_out.at[mb, k],
            dst_ref=z_in.at[mb, k],
            send_sem=zr_ss.at[mb, k],
            recv_sem=zr_rs.at[mb, k],
            device_id=(seg, z_mate),
            device_id_type=MESH,
        )

    def shift(mb, k):
        out = rise_out if mb == 0 else fall_out
        return pltpu.make_async_remote_copy(
            src_ref=finished.at[mb, k],
            dst_ref=out.at[0, :, pl.ds(k * width, width)],
            send_sem=y_ss.at[mb, k],
            recv_sem=y_rs.at[mb, k],
            device_id=(seg_up if mb == 0 else seg_down, me),
            device_id_type=MESH,
        )

    def detour(mb, k):
        return pltpu.make_async_remote_copy(
            src_ref=finished.at[mb, k],
            dst_ref=passing.at[mb, k],
            send_sem=y_ss.at[mb, k],
            recv_sem=pass_rs.at[mb, k],
            device_id=(seg_base + DETOURS[mb][k], me),
            device_id_type=MESH,
        )

    def onward(mb, k):
        out = rise_out if mb == 0 else fall_out
        return pltpu.make_async_remote_copy(
            src_ref=passing.at[mb, k],
            dst_ref=out.at[0, :, pl.ds(k * width, width)],
            send_sem=pass_ss.at[mb, k],
            recv_sem=y_rs.at[mb, k],
            device_id=(past_edge[mb], me),
            device_id_type=MESH,
        )

    ids_exchange = [
        pltpu.make_async_remote_copy(
            src_ref=source,
            dst_ref=ids_land.at[mb],
            send_sem=ids_ss.at[mb],
            recv_sem=ids_rs.at[mb],
            device_id=(seg, z_mate),
            device_id_type=MESH,
        )
        for mb, source in enumerate((rise_ids, fall_ids))
    ]

    def normalize(mb):
        @pl.loop(0, blocks)
        def _(b):
            at = pl.ds(pl.multiple_of(b * BR, BR), BR)
            value = acts[mb, at, :].astype(F32)
            scale = lax.rsqrt(jnp.mean(value * value, axis=-1, keepdims=True) + EPS)
            for k in range(CHUNKS):
                cut = slice(k * width, (k + 1) * width)
                normed[mb, k, at, :] = (value[:, cut] * scale * gain_ref[:, cut]).astype(BF16)

    def codes(s, ids):
        mb = s % 2
        named = [[ids[mb][j, b] for j in range(2)] for b in range(blocks)]
        code = []
        for b in range(blocks):
            code.append([])
            for j in range(2):
                slot = jnp.int32(0)
                for earlier in range(b):
                    for other in range(2):
                        slot = slot + (named[earlier][other] == named[b][j]).astype(jnp.int32)
                code[b].append(2 * named[b][j] + slot)
        return named, code

    def set_picker(s, ids):
        _, code = codes(s, ids)
        row = lax.broadcasted_iota(jnp.int32, (half, rows), 0)
        column = lax.broadcasted_iota(jnp.int32, (half, rows), 1)
        same = (row % BR == column % BR).astype(F32)
        total = jnp.zeros((half, rows), F32)
        for j in range(2):
            wanted = jnp.zeros((half, rows), jnp.int32)
            for b in range(blocks):
                wanted = wanted + (column // BR == b).astype(jnp.int32) * code[b][j]
            total = total + (row // BR == wanted).astype(F32)
        picker[s] = (total * same).astype(BF16)

    def pick(s, k):
        source = normed if s < 2 else far_normed
        chosen = jnp.dot(picker[s], source[s % 2, k], preferred_element_type=F32)
        sending[s, k] = chosen.astype(BF16)
        own = pl.ds(pl.multiple_of(x * pick_rows, pick_rows), pick_rows)
        mine = pl.ds(pl.multiple_of(own_half + x * pick_rows, pick_rows), pick_rows)
        arrived[s, k, mine, :] = sending[s, k, own, :]
        for i in FAR_FIRST:
            x_forward(s, k, i).start()

    def relay(s, k):
        z_forward(s % 2, k).wait_recv()
        pick(s, k)

    def gates(s, ids):
        source = normed if s < 2 else far_normed
        mb = s % 2

        @pl.loop(0, blocks)
        def _(b):
            at = pl.ds(pl.multiple_of(b * BR, BR), BR)
            sums = [jnp.zeros((BR, LANES), F32) for _ in range(EXPERTS)]
            for k in range(CHUNKS):
                for t in range(tiles):
                    value = source[mb, k, at, t * LANES : (t + 1) * LANES].astype(F32)
                    first = k * width + t * LANES
                    for e in range(EXPERTS):
                        sums[e] = sums[e] + value * router_ref[e : e + 1, first : first + LANES]
            for e in range(EXPERTS):
                total = jnp.sum(sums[e], axis=-1, keepdims=True)
                scores[e, at, :] = jnp.broadcast_to(jax.nn.sigmoid(total), (BR, LANES))

        named, code = codes(s, ids)
        column = lax.broadcasted_iota(jnp.int32, (BR, LANES), 1)
        row = lax.broadcasted_iota(jnp.int32, (BR, LANES), 0)
        same = (column % BR == row).astype(F32)
        for b in range(blocks):
            at = slice(b * BR, (b + 1) * BR)
            score = []
            for j in range(2):
                value = jnp.zeros((BR, LANES), F32)
                for e in range(EXPERTS):
                    value = value + scores[e, at, :] * (named[b][j] == e).astype(F32)
                score.append(value)
            total = score[0] + score[1]
            for first in range(0, half, LANES):
                place = (column + first) // BR
                value = jnp.zeros((BR, LANES), F32)
                for j in range(2):
                    value = value + (place == code[b][j]).astype(F32) * same * (score[j] / total)
                main = value.astype(BF16)
                mixer[s, at, first : first + LANES] = main
                mixer_rest[s, at, first : first + LANES] = (value - main.astype(F32)).astype(BF16)

    def to_core(s, k):
        for i in range(1, XN):
            x_forward(s, k, i).wait_recv()
        core_forward(s, k).start()

    def experts(s):
        for k in range(CHUNKS):
            core_forward(s, k).wait_recv()
            core_forward(s, k).wait_send()

        @pl.loop(0, 2)
        def _(t):
            at = pl.ds(pl.multiple_of(t * half, half), half)
            gate_pre = jnp.zeros((half, units), F32)
            up_pre = jnp.zeros((half, units), F32)
            for k in range(CHUNKS):
                value = arrived[s, k, at, :]
                cut = slice(k * width, (k + 1) * width)
                gate_pre = gate_pre + jnp.dot(value, gate_w[cut, :], preferred_element_type=F32)
                up_pre = up_pre + jnp.dot(value, up_w[cut, :], preferred_element_type=F32)
            hidden[at, :] = (jax.nn.silu(gate_pre) * up_pre).astype(BF16)

        @pl.loop(0, CHUNKS)
        def _(k):
            for first in (mate_half, own_half):
                at = pl.ds(first, half)
                part = jnp.dot(hidden[at, :], down_w[k], preferred_element_type=F32)
                arrived[s, k, at, :] = part.astype(BF16)
                if first is mate_half:
                    core_part(s, k).start()

    def pair_sum(s, k):
        core_part(s, k).wait_recv()

        @pl.loop(0, XN)
        def _(i):
            at = pl.ds(pl.multiple_of(i * pick_rows, pick_rows), pick_rows)
            mine = pl.ds(pl.multiple_of(own_half + i * pick_rows, pick_rows), pick_rows)
            total = arrived[s, k, mine, :].astype(F32) + core_sum[s, k, at, :].astype(F32)
            arrived[s, k, mine, :] = total.astype(BF16)

        here = pl.ds(pl.multiple_of(x * pick_rows, pick_rows), pick_rows)
        mine = pl.ds(pl.multiple_of(own_half + x * pick_rows, pick_rows), pick_rows)
        returned[s, k, here, :] = arrived[s, k, mine, :]

    def send_back(s, k):
        for i in FAR_FIRST:
            x_return(s, k, i).start()

    def weighted(s, k):
        value = returned[s, k]
        return jnp.dot(mixer[s], value, preferred_element_type=F32) + jnp.dot(
            mixer_rest[s], value, preferred_element_type=F32
        )

    def combine(s, k):
        mb = s % 2
        for i in range(1, XN):
            x_return(s, k, i).wait_recv()
        z_out[mb, k] = weighted(s, k).astype(BF16)
        z_return(mb, k).start()

    def finish(mb, k):
        for i in range(1, XN):
            x_return(mb, k, i).wait_recv()
        z_return(mb, k).wait_recv()
        total = weighted(mb, k) + z_in[mb, k].astype(F32)
        mixed = acts[mb, :, k * width : (k + 1) * width].astype(F32) + ROUTE_SCALE * total
        finished[mb, k] = mixed.astype(BF16)
        if k < len(DETOURS[mb]):

            @pl.when(at_edge[mb])
            def _():
                detour(mb, k).start()

            @pl.when(jnp.logical_not(at_edge[mb]))
            def _():
                shift(mb, k).start()

        else:
            shift(mb, k).start()

    def pass_on(mb, k):
        if k >= len(DETOURS[mb]):
            return

        @pl.when(y == DETOURS[mb][k])
        def _():
            detour(mb, k).wait_recv()
            onward(mb, k).start()

    act_copies = [
        pltpu.make_async_copy(source.at[0], acts.at[mb], act_sem.at[mb])
        for mb, source in enumerate((rise_hbm, fall_hbm))
    ]
    weight_copies = [
        pltpu.make_async_copy(gate_hbm.at[0], gate_w, w_sem.at[0]),
        pltpu.make_async_copy(up_hbm.at[0], up_w, w_sem.at[1]),
    ] + [
        pltpu.make_async_copy(down_hbm.at[0, :, pl.ds(k * width, width)], down_w.at[k], dw_sem.at[k])
        for k in range(CHUNKS)
    ]
    ids_own = (ids_rise, ids_fall)
    ids_far = (far_rise_ids, far_fall_ids)
    ids_copies = [
        pltpu.make_async_copy(source, ids_own[mb], ids_sem.at[mb])
        for mb, source in enumerate((rise_ids, fall_ids))
    ]
    ids_far_copies = [
        pltpu.make_async_copy(ids_land.at[mb], ids_far[mb], ids_sem.at[2 + mb]) for mb in range(2)
    ]
    act_copies[0].start()
    for copy in ids_copies:
        copy.start()
    act_copies[1].start()

    barrier = pltpu.get_barrier_semaphore()
    partners = [(seg, x_device(i)) for i in range(1, XN)]
    partners += [(seg, z_mate), (seg, core_mate), (base_up, me), (base_down + YN - 1, me)]
    partners += [(seg_base + lax.rem(y + j, YN), me) for j in range(1, YN)]

    def greet(partner):
        pl.semaphore_signal(barrier, inc=1, device_id=partner, device_id_type=MESH)

    for partner in partners:
        greet(partner)

    @pl.when(at_edge[1])
    def _():
        for j in range(YN - 1):
            greet((base_down + j, me))

    @pl.when(at_edge[0])
    def _():
        for j in range(1, YN):
            greet((base_up + j, me))

    at_either = jnp.logical_or(at_edge[0], at_edge[1]).astype(jnp.int32)

    act_copies[0].wait()
    normalize(0)
    for copy in weight_copies:
        copy.start()
    for copy in ids_copies:
        copy.wait()
    set_picker(0, ids_own)
    pl.semaphore_wait(barrier, len(partners) + (YN - 1) * at_either)

    every = range(CHUNKS)
    rise, fall, far_rise, far_fall = range(4)
    for copy in ids_exchange:
        copy.start()
    for k in every:
        z_forward(0, k).start()
    for k in every:
        pick(rise, k)
    set_picker(fall, ids_own)
    act_copies[1].wait()
    normalize(1)
    for k in every:
        z_forward(1, k).start()
    gates(rise, ids_own)
    for copy in ids_exchange:
        copy.wait()
    for copy in ids_far_copies:
        copy.start()
    for copy in ids_far_copies:
        copy.wait()
    set_picker(far_rise, ids_far)
    set_picker(far_fall, ids_far)
    to_core(rise, 0)
    relay(far_rise, 0)
    pick(fall, 0)
    for k in every[1:]:
        to_core(rise, k)
    for copy in weight_copies:
        copy.wait()
    pick(fall, 1)
    experts(rise)
    for k in every[1:]:
        relay(far_rise, k)
        if k + 1 < CHUNKS:
            pick(fall, k + 1)
    for k in every:
        pair_sum(rise, k)
    gates(fall, ids_own)
    for k in every:
        to_core(far_rise, k)
        to_core(fall, k)
    for k in every[: FILL[0]]:
        send_back(rise, k)
    experts(far_rise)
    for k in every:
        pair_sum(far_rise, k)
        send_back(far_rise, k)
    gates(far_rise, ids_far)
    for k in every[: CHUNKS // 2]:
        relay(far_fall, k)
    experts(fall)
    for k in every:
        pair_sum(fall, k)
    for k in every[: CHUNKS // 2]:
        combine(far_rise, k)
    for k in every[CHUNKS // 2 :]:
        relay(far_fall, k)
        combine(far_rise, k)
    gates(far_fall, ids_far)
    for k in every[FILL[0] : FILL[1]]:
        send_back(rise, k)
    for k in every:
        to_core(far_fall, k)
        if 1 <= k <= FILL[0]:
            finish(0, k - 1)
    for k in every[: FILL[0]]:
        pass_on(0, k)
    experts(far_fall)
    for k in every:
        pair_sum(far_fall, k)
        send_back(far_fall, k)
    late = list(every[FILL[1] :])
    for k in every:
        send_back(fall, k)
        if k < len(late):
            send_back(rise, late[k])
    for k in every[FILL[0] : FILL[1]]:
        finish(0, k)
    for k in every:
        combine(far_fall, k)
        if FILL[0] <= k < FILL[1]:
            pass_on(0, k)
    last = []
    for k in every:
        last.append((1, k))
        if k < len(late):
            last.append((0, late[k]))
    waiting = []
    for mb, k in last:
        finish(mb, k)
        while waiting and waiting[0][2] <= 1:
            pass_on(*waiting.pop(0)[:2])
        waiting = [(*step, lag - 1) for *step, lag in waiting]
        waiting.append((mb, k, 1 if mb == 1 and k >= 2 else 2))
    for mb, k, _ in waiting:
        pass_on(mb, k)

    for k in every:
        for mb in range(2):
            z_forward(mb, k).wait_send()
            z_return(mb, k).wait_send()
            shift(mb, k).wait_send()
        for s in range(4):
            core_part(s, k).wait_send()
            for i in range(1, XN):
                x_forward(s, k, i).wait_send()
                x_return(s, k, i).wait_send()
    for mb in range(2):
        for k, by in enumerate(DETOURS[mb]):

            @pl.when(y == by)
            def _():
                onward(mb, k).wait_send()

    for k in every:
        for mb in range(2):
            shift(mb, k).wait_recv()


def on_device(
    rising_acts,
    falling_acts,
    norm_gain,
    router_weight,
    gate_weight,
    up_weight,
    down_weight,
    rising_ids,
    falling_ids,
):
    rows, features = rising_acts.shape[1:]
    units = gate_weight.shape[2]
    width = features // CHUNKS
    half = XN * 2 * BR
    segments = lax.axis_size("segment")
    top, blocks = rising_ids.shape[2], rising_ids.shape[1]
    dma = pltpu.SemaphoreType.DMA
    hbm = pl.BlockSpec(memory_space=pl.ANY)
    vmem = pl.BlockSpec(memory_space=pltpu.VMEM)
    result = jax.ShapeDtypeStruct(rising_acts.shape, BF16)
    return pl.pallas_call(
        functools.partial(relay_kernel, rows, features, units, segments),
        out_shape=(result, result),
        in_specs=[hbm, hbm, vmem, vmem, hbm, hbm, hbm, hbm, hbm],
        out_specs=(hbm, hbm),
        scratch_shapes=[
            pltpu.VMEM((2, rows, features), BF16),
            pltpu.VMEM((features, units), BF16),
            pltpu.VMEM((features, units), BF16),
            pltpu.VMEM((CHUNKS, units, width), BF16),
            pltpu.VMEM((2, top, blocks), jnp.int32),
        ]
        + [pltpu.SMEM((top, blocks), jnp.int32)] * 4
        + [
            pltpu.VMEM((4, half, rows), BF16),
            pltpu.VMEM((4, rows, half), BF16),
            pltpu.VMEM((4, rows, half), BF16),
            pltpu.VMEM((2, CHUNKS, rows, width), BF16),
            pltpu.VMEM((2, CHUNKS, rows, width), BF16),
            pltpu.VMEM((4, CHUNKS, half, width), BF16),
            pltpu.VMEM((4, CHUNKS, 2 * half, width), BF16),
            pltpu.VMEM((2 * half, units), BF16),
            pltpu.VMEM((4, CHUNKS, half, width), BF16),
            pltpu.VMEM((4, CHUNKS, half, width), BF16),
            pltpu.VMEM((2, CHUNKS, rows, width), BF16),
            pltpu.VMEM((2, CHUNKS, rows, width), BF16),
            pltpu.VMEM((2, CHUNKS, rows, width), BF16),
            pltpu.VMEM((EXPERTS, rows, LANES), F32),
            dma((2,)),
            dma((2,)),
            dma((CHUNKS,)),
            dma((4,)),
            dma((2,)),
            dma((2,)),
            dma((2, CHUNKS)),
            dma((2, CHUNKS)),
            dma((4, CHUNKS, XN - 1)),
            dma((4, CHUNKS, XN - 1)),
            dma((4, CHUNKS)),
            dma((4, CHUNKS)),
            dma((4, CHUNKS)),
            dma((4, CHUNKS)),
            dma((4, CHUNKS, XN - 1)),
            dma((4, CHUNKS, XN - 1)),
            dma((2, CHUNKS)),
            dma((2, CHUNKS)),
            dma((2, CHUNKS)),
            dma((2, CHUNKS)),
            pltpu.VMEM((2, len(DETOURS[0]), rows, width), BF16),
            dma((2, CHUNKS)),
            dma((2, CHUNKS)),
        ],
        compiler_params=pltpu.CompilerParams(
            collective_id=0, has_side_effects=True, vmem_limit_bytes=60 << 20
        ),
        name="relay",
    )(
        rising_acts,
        falling_acts,
        norm_gain,
        router_weight[0].T,
        gate_weight,
        up_weight,
        down_weight,
        rising_ids[0].T,
        falling_ids[0].T,
    )


def solution(mesh):
    return jax.shard_map(
        on_device,
        mesh=mesh,
        in_specs=(
            P("segment", "expert", None),
            P("segment", "expert", None),
            P("segment", None),
            P("segment", None, None),
            P("segment", None, "expert"),
            P("segment", None, "expert"),
            P("segment", "expert", None),
            P("segment", "expert", None),
            P("segment", "expert", None),
        ),
        out_specs=(P("segment", "expert", None), P("segment", "expert", None)),
        check_vma=False,
    )
```
